256 devices in a mesh: seq: 64 (over x, z, core), head: 4 (over y).
Axes of the slice: x: 4, y: 4, z: 8, core: 2. Of those that a mesh axis runs over, the one named last changes fastest.
Arguments:
- query_rows: bfloat16 [32768, 2048], P('seq', 'head'), may hold values from -6 to 6
- key_rows: bfloat16 [32768, 2048], P('seq', 'head'), may hold values from -6 to 6
- value_rows: bfloat16 [32768, 4096], P('seq', 'head'), may hold values from -6 to 6
- out_grad: bfloat16 [32768, 3072], P('seq', 'head'), may hold values from -6 to 6
- out_weight: bfloat16 [4096, 3072], P('head'), may hold values from -0.109375 to 0.109375
- level_codes: int32 [12, 32, 32768], P(None, 'head', 'seq'), may hold values from 0 to 15
- level_table: float32 [32, 16], P('head'), may hold values from 0.1 to 1
Outputs:
- query_grad: bfloat16 [32768, 2048], P('seq', 'head')
- key_grad: bfloat16 [32768, 2048], P('seq', 'head')
- value_grad: bfloat16 [32768, 4096], P('seq', 'head')
The draws below stay inside these ranges and needn't reach their ends.
All inputs are finite; a program needn't handle non-finite values.
Results may differ from the reference program's by a relative error of at most 0.0062.
Values may be sent and summed in bfloat16 or wider, within the bound.
A program may use at most 128 MiB of HBM per device.

```python
import math
import jax
import jax.numpy as jnp
from jax import lax

D = 3072
HEADS = 32
DK = 64
DV = 128
BLK = 64
LEVELS = 12
TABLE = 16
TOK_DEV = 512
TOKENS = 32768
N_SEQ = 64


def with_ends(entries, own_key, low, top_value):
    spot = [jax.random.randint(jax.random.fold_in(own_key, axis), (), 0, length) for axis, length in enumerate(entries.shape)]
    main_axis = entries.shape.index(max(entries.shape))
    next_to = spot[:main_axis] + [(spot[main_axis] + 1) % entries.shape[main_axis]] + spot[main_axis + 1:]
    return entries.at[tuple(spot)].set(low).at[tuple(next_to)].set(top_value)


def steps_of(stream_key, extent, split, least, largest):
    factor_of, own = 1.0, jax.random.fold_in(stream_key, 6)
    for dim, shards_of in split:
        steps = jnp.exp(jax.random.uniform(jax.random.fold_in(own, dim), (shards_of,), jnp.float32, least / len(split), largest / len(split)))
        factor_of = factor_of * jnp.repeat(steps, extent[dim] // shards_of).reshape([-1 if axis == dim else 1 for axis in range(len(extent))])
    return factor_of


def noise(rng, shape, spread, most, cuts=(), kind=jnp.bfloat16):
    loudness = steps_of(rng, shape, cuts, -0.22, 0.18) if cuts else 1.0
    array = jax.random.normal(rng, shape, jnp.float32) * spread * loudness
    return jnp.minimum(jnp.maximum(array, -most), most).astype(kind)


def setup_inputs(seed: int = 0) -> dict:
    seeds = jax.random.split(jax.random.key(seed), 8)
    return {
        "query_rows": noise(seeds[0], (TOKENS, HEADS * DK), 1.0, 6.0, ((0, 64), (1, 4))),
        "key_rows": noise(seeds[1], (TOKENS, HEADS * DK), 1.0, 6.0, ((0, 64), (1, 4))),
        "value_rows": noise(seeds[2], (TOKENS, HEADS * DV), 1.0, 6.0, ((0, 64), (1, 4))),
        "out_grad": noise(seeds[3], (TOKENS, D), 1.0, 6.0, ((0, 64), (1, 4))),
        "out_weight": noise(seeds[4], (HEADS * DV, D), D ** -0.5, 0.109375, ((0, 4),)),
        "level_codes": with_ends(jax.random.randint(seeds[5], (LEVELS, HEADS, TOKENS), 0, TABLE), jax.random.fold_in(seeds[5], 1), 0, TABLE - 1).astype(jnp.int32),
        "level_table": jnp.clip(jnp.exp(math.log(1.0) - 2.3025851 * jax.random.uniform(seeds[6], (HEADS, TABLE), jnp.float32) ** steps_of(seeds[6], (HEADS, TABLE), ((0, 4),), -0.2, 0.2)), 0.1, 1.0),
    }


def level_scales():
    span_list = [DK * BLK * 2 ** max(level - 1, 0) for level in range(LEVELS)]
    return jnp.asarray([span ** -0.5 for span in span_list], dtype=jnp.float32)


def depth_table(row_count, bit_count):
    block_id = jnp.arange(row_count, dtype=jnp.int32) // BLK
    crossed = jnp.bitwise_xor(block_id[:, None], block_id[None, :])
    depth_map = jnp.zeros((row_count, row_count), jnp.int32)
    for exponent in range(bit_count):
        depth_map = depth_map + (crossed >= 2 ** exponent).astype(jnp.int32)
    return depth_map


def member_table(count, bit_count):
    target = jnp.arange(count, dtype=jnp.int32)[:, None]
    source = jnp.arange(count, dtype=jnp.int32)[None, :]
    crossed = jnp.bitwise_xor(target, source)
    below = source < target
    planes = [jnp.logical_and(below, jnp.logical_and(crossed >= 2 ** level, crossed < 2 ** (level + 1))) for level in range(bit_count)]
    return jnp.stack(planes, axis=-1).astype(jnp.float32)


def group_terms(query, key_product, value_product, dgrad, weights, depth_map, low_bits):
    row_count = query.shape[0]
    places = jnp.arange(row_count, dtype=jnp.int32)
    causal = places[:, None] >= places[None, :]
    mixing = jnp.zeros((HEADS, row_count, row_count), jnp.float32)
    for level in range(low_bits + 1):
        chosen = jnp.logical_and(depth_map == level, causal)
        mixing = mixing + jnp.where(chosen[None], weights[level][:, :, None], jnp.zeros((), jnp.float32))
    top_level_index = lax.Precision.HIGHEST
    query_f = query.astype(jnp.float32)
    key_product_float = key_product.astype(jnp.float32)
    value_product_float = value_product.astype(jnp.float32)
    dgrad_f = dgrad.astype(jnp.float32)
    scores = jnp.einsum("thk,shk->hts", query_f, key_product_float, precision=top_level_index)
    grads = jnp.einsum("thv,shv->hts", dgrad_f, value_product_float, precision=top_level_index)
    grad_mix = (mixing * grads).astype(jnp.bfloat16).astype(jnp.float32)
    score_mix = (mixing * scores).astype(jnp.bfloat16).astype(jnp.float32)
    query_local = jnp.einsum("hts,shk->thk", grad_mix, key_product_float, precision=top_level_index)
    key_local = jnp.einsum("hts,thk->shk", grad_mix, query_f, precision=top_level_index)
    value_local = jnp.einsum("hts,thv->shv", score_mix, dgrad_f, precision=top_level_index)
    local_level_state = jnp.einsum("qrg,qri->rgi", key_product_float, value_product_float, precision=top_level_index)
    return query_local, key_local, value_local, local_level_state


def reference(query_rows, key_rows, value_rows, out_grad, out_weight, level_codes, level_table):
    groups = N_SEQ
    low_bits = (TOK_DEV // BLK).bit_length() - 1
    seq_bits = N_SEQ.bit_length() - 1
    top_level_index = lax.Precision.HIGHEST
    dout = jnp.dot(out_grad, out_weight.T, preferred_element_type=jnp.float32).astype(jnp.bfloat16)
    head_ids = jnp.arange(HEADS, dtype=jnp.int32)
    looked = level_table[head_ids[None, :, None], level_codes]
    weights = looked * level_scales()[:, None, None]
    query = query_rows.reshape(groups, TOK_DEV, HEADS, DK)
    key_product = key_rows.reshape(groups, TOK_DEV, HEADS, DK)
    value_product = value_rows.reshape(groups, TOK_DEV, HEADS, DV)
    dgrad = dout.reshape(groups, TOK_DEV, HEADS, DV)
    weight_blocks = weights.reshape(LEVELS, HEADS, groups, TOK_DEV).transpose(2, 0, 1, 3)
    depth_map = depth_table(TOK_DEV, low_bits)

    def local_part(items):
        return group_terms(items[0], items[1], items[2], items[3], items[4], depth_map, low_bits)

    query_local, key_local, value_local, own_states = lax.map(local_part, (query, key_product, value_product, dgrad, weight_blocks))
    member = member_table(groups, seq_bits)
    remote_weights = weight_blocks[:, low_bits + 1:low_bits + 1 + seq_bits]
    group_ids = jnp.arange(groups, dtype=jnp.int32)
    bit_ids = jnp.arange(seq_bits, dtype=jnp.int32)
    upper_bits = jnp.bitwise_and(jnp.right_shift(group_ids[:, None], bit_ids[None, :]), 1).astype(jnp.float32)

    def remote_part(items):
        member_row, query_g, dout_g, weight_g, upper = items
        states = jnp.einsum("jb,jhkv->bhkv", member_row, own_states, precision=top_level_index)
        state_low = states.astype(jnp.bfloat16).astype(jnp.float32)
        readout = jnp.einsum("thv,bhkv->bthk", dout_g.astype(jnp.float32), state_low, precision=top_level_index)
        query_remote = jnp.sum(readout * weight_g.transpose(0, 2, 1)[..., None], axis=0)
        factor = (weight_g * upper[:, None, None]).transpose(0, 2, 1)[..., None]
        scaled = (factor * query_g.astype(jnp.float32)[None]).astype(jnp.bfloat16).astype(jnp.float32)
        level_grad = jnp.einsum("bthk,thv->bhkv", scaled, dout_g.astype(jnp.float32), precision=top_level_index)
        return query_remote, level_grad

    query_remote, per_level_gradient = lax.map(remote_part, (member, query, dgrad, remote_weights, upper_bits))

    def collect_back(column_slot):
        return jnp.einsum("ns,nsrqm->rqm", column_slot, per_level_gradient, precision=top_level_index)

    returned = lax.map(collect_back, member.transpose(1, 0, 2))
    returned_lower_part = returned.astype(jnp.bfloat16).astype(jnp.float32)
    key_remote = jnp.einsum("gthv,ghkv->gthk", value_product.astype(jnp.float32), returned_lower_part, precision=top_level_index)
    value_remote = jnp.einsum("gthk,ghkv->gthv", key_product.astype(jnp.float32), returned_lower_part, precision=top_level_index)
    query_grad = (query_local + query_remote).astype(jnp.bfloat16).reshape(TOKENS, HEADS * DK)
    key_grad = (key_local + key_remote).astype(jnp.bfloat16).reshape(TOKENS, HEADS * DK)
    value_grad = (value_local + value_remote).astype(jnp.bfloat16).reshape(TOKENS, HEADS * DV)
    return (query_grad, key_grad, value_grad)
```

```python
import jax
import jax.numpy as jnp
from jax import lax
from jax.experimental import pallas as pl
from jax.experimental.pallas import tpu as pltpu
from jax.sharding import PartitionSpec as P

DK = 64
DV = 128
BLK = 64
LB = 3
SEQ_BITS = 6
ROWS = 512
HEADS = 8
PAIRS = 4
FEAT = 768
CHUNKS = 4
CROWS = ROWS // CHUNKS
HALF = 256
SLICE = 32
SCALES = [float((DK * BLK * 2 ** max(level - 1, 0)) ** -0.5) for level in range(LB + 1 + SEQ_BITS)]

F32 = jnp.float32
BF16 = jnp.bfloat16

S0, S1, S2, S4, R0, R1, R2, R3, R4, N_SEM = 0, 1, 8, 11, 12, 14, 21, 24, 31, 32


def nt(a, b):
    return lax.dot_general(a, b, (((1,), (1,)), ((), ())), preferred_element_type=F32)


def nn(a, b):
    return lax.dot_general(a, b, (((1,), (0,)), ((), ())), preferred_element_type=F32)


def flipped(value, mask, bits):
    out = value
    for k in range(bits):
        if mask >> k & 1:
            out = out + (1 - 2 * ((value // 2**k) % 2)) * 2**k
    return out


def kernel(
    q_hbm, k_hbm, v_hbm, og_hbm, w_hbm, codes_ref, table_ref,
    qo_hbm, ko_hbm, vo_hbm,
    qp, kp, vp, w4, gath, dout, kT, qT, lam, inner, sm,
    gsb, pgs, zbuf, xbuf, state_low,
    lg, rb0, rbh, rsrc, rbuf, tsrc, tbuf, rets, rfin,
    kacc, vacc, qo, ko, vo,
    loc_sem, out_sem, ys, yr, ss, sr,
):
    g = lax.axis_index("seq")
    y = lax.axis_index("head")
    c = g % 2
    z = (g // 2) % 8
    x = g // 16
    right, left, across = (y + 1) % 4, (y + 3) % 4, (y + 2) % 4

    def z_peer(i):
        return (x * 16 + flipped(z, i, 3) * 2 + c, y)

    def x_peer(i):
        return (flipped(x, i, 2) * 16 + z * 2 + c, y)

    partner = (g + 1 - 2 * c, y)
    peers = [partner, (g, right), (g, left)]
    peers += [z_peer(i) for i in range(1, 8)] + [x_peer(i) for i in range(1, 4)]

    loads = []
    for p in range(PAIRS):
        loads.append(pltpu.make_async_copy(k_hbm.at[:, pl.ds(p * 128, 128)], kp.at[p], loc_sem.at[len(loads)]))
    for p in range(PAIRS):
        loads.append(pltpu.make_async_copy(v_hbm.at[:, pl.ds(p * 256, 256)], vp.at[p], loc_sem.at[len(loads)]))
    for p in range(PAIRS):
        loads.append(pltpu.make_async_copy(q_hbm.at[:, pl.ds(p * 128, 128)], qp.at[p], loc_sem.at[len(loads)]))
    loads.append(pltpu.make_async_copy(og_hbm, gath.at[y], loc_sem.at[len(loads)]))
    for p in range(4):
        loads.append(pltpu.make_async_copy(w_hbm.at[:, pl.ds(p * FEAT, FEAT)], w4.at[p], loc_sem.at[len(loads)]))
    for load in loads:
        load.start()

    barrier = pltpu.get_barrier_semaphore()
    for peer in peers:
        pl.semaphore_signal(barrier, inc=1, device_id=peer, device_id_type=pl.DeviceIdType.MESH)
    pl.semaphore_wait(barrier, len(peers))

    def remote(src, dst, send, recv, slot, to):
        return pltpu.make_async_remote_copy(
            src_ref=src, dst_ref=dst, send_sem=send.at[slot], recv_sem=recv.at[slot],
            device_id=to, device_id_type=pl.DeviceIdType.MESH,
        )

    def own(j):
        rows = pl.ds(j * CROWS, CROWS)
        return [
            remote(og_hbm.at[rows], gath.at[y, rows], ys, yr, j, (g, right)),
            remote(og_hbm.at[rows], gath.at[y, rows], ys, yr, 4 + j, (g, left)),
        ]

    def forward(j):
        first = pl.ds(j * CROWS, CROWS // 2)
        second = pl.ds(j * CROWS + CROWS // 2, CROWS // 2)
        return [
            remote(gath.at[left, first], gath.at[left, first], ys, yr, 8 + j, (g, right)),
            remote(gath.at[right, second], gath.at[right, second], ys, yr, 12 + j, (g, left)),
        ]

    def start(copies):
        for copy in copies:
            copy.start()
        sent.extend(copies)
        return copies

    def arrive(copies):
        for copy in copies:
            copy.wait_recv()

    sent = []
    owns = [own(j) for j in range(CHUNKS)]
    forwards = [forward(j) for j in range(CHUNKS)]
    start(owns[0])
    start(owns[1])

    for load in loads[:8]:
        load.wait()

    def states_of(p, _):
        kT[p] = kp[p].T
        both = nn(kT[p], vp[p])
        at = pl.multiple_of(p * 128, 128)
        gsb[pl.ds(at, 64), :] = both[:64, :128]
        gsb[pl.ds(at + 64, 64), :] = both[64:, 128:]
        return 0

    lax.fori_loop(0, PAIRS, states_of, 0)
    s0 = start([remote(gsb, pgs, ss, sr, S0, partner)])

    table = table_ref[...]
    columns = [jnp.broadcast_to(table[:, j:j + 1], (HEADS, ROWS)) for j in range(16)]
    for level in range(LB + 1 + SEQ_BITS):
        codes = codes_ref[level]
        looked = jnp.zeros((HEADS, ROWS), F32)
        for j in range(16):
            looked = jnp.where(codes == j, columns[j], looked)
        looked = looked * SCALES[level]
        if level > LB:
            looked = looked * ((g // 2 ** (level - LB - 1)) % 2).astype(F32)
        lam[level] = looked
    token_block = lax.broadcasted_iota(jnp.int32, (HEADS, ROWS), 1) // BLK
    for cs in range(ROWS // BLK):
        line = jnp.zeros((HEADS, ROWS), F32)
        for ct in range(cs, ROWS // BLK):
            line = jnp.where(token_block == ct, lam[(ct ^ cs).bit_length()], line)
        inner[cs] = line

    for load in loads[8:12]:
        load.wait()

    def turned(p, _):
        qT[p] = qp[p].T
        return 0

    lax.fori_loop(0, PAIRS, turned, 0)

    mine = pl.ds(pl.multiple_of(c * HALF, HALF), HALF)
    other = pl.ds(pl.multiple_of((1 - c) * HALF, HALF), HALF)
    arrive(s0)
    zbuf[0] = (gsb[mine, :] + pgs[mine, :]).astype(BF16)
    s1 = start([remote(zbuf.at[0], zbuf.at[i], ss, sr, S1 + i - 1, z_peer(i)) for i in range(1, 8)])
    state_low[0] = pgs[...].astype(BF16)

    def turn(j):
        arrive(owns[j])
        start(forwards[j])
        if j + 2 < CHUNKS:
            start(owns[j + 2])

    def mix_of(h, s0_, count, t0_, width):
        lines = [
            jnp.broadcast_to(inner[s0_ // BLK + i, pl.ds(h, 1), pl.ds(t0_, width)], (BLK, width))
            for i in range(count // BLK)
        ]
        mix = jnp.concatenate(lines, axis=0)
        s_at = lax.broadcasted_iota(jnp.int32, (count, width), 0) + s0_
        t_at = lax.broadcasted_iota(jnp.int32, (count, width), 1) + t0_
        return jnp.where(s_at <= t_at, mix, 0.0)

    def masked(pair, e):
        lane = lax.broadcasted_iota(jnp.int32, pair.shape, 1)
        return jnp.where((lane >= 64) == (e == 1), pair, jnp.zeros_like(pair))

    def scores_of(p, _):
        for e in range(2):
            h = 2 * p + e
            keys = masked(kp[p], e)
            query = qp[p]
            sm[h, pl.ds(0, HALF), :] = (mix_of(h, 0, HALF, 0, ROWS) * nt(keys[:HALF], query)).astype(BF16)
            sm[h, pl.ds(HALF, HALF), pl.ds(HALF, HALF)] = (
                mix_of(h, HALF, HALF, HALF, HALF) * nt(keys[HALF:], query[HALF:])
            ).astype(BF16)
        return 0

    turn(0)
    lax.fori_loop(0, 2, scores_of, 0)
    turn(1)
    lax.fori_loop(2, 4, scores_of, 0)

    arrive(s1)
    parts = [zbuf[i].astype(F32) for i in range(8)]
    pair1 = parts[2] + parts[3]
    quad = (parts[4] + parts[5]) + (parts[6] + parts[7])
    xbuf[0] = ((parts[0] + parts[1]) + pair1 + quad).astype(BF16)
    s2 = start([remote(xbuf.at[0], xbuf.at[i], ss, sr, S2 + i - 1, x_peer(i)) for i in range(1, 4)])
    state_low[1, mine, :] = zbuf[1]
    state_low[2, mine, :] = pair1.astype(BF16)
    state_low[3, mine, :] = quad.astype(BF16)

    turn(2)
    arrive(s2)
    state_low[4, mine, :] = xbuf[1]
    state_low[5, mine, :] = (xbuf[2].astype(F32) + xbuf[3].astype(F32)).astype(BF16)
    s4 = start([remote(state_low.at[pl.ds(1, 5), mine], state_low.at[pl.ds(1, 5), mine], ss, sr, S4, partner)])

    for load in loads[12:]:
        load.wait()
    arrive(forwards[0])
    arrive(forwards[1])

    def project(first):
        def tile(n, _):
            cols = pl.ds(pl.multiple_of(n * 256, 256), 256)
            total = None
            for d in range(4):
                part = nt(gath[d, pl.ds(first, HALF), :], w4[d, cols, :])
                total = part if total is None else total + part
            low = total.astype(BF16)
            dout[2 * n, pl.ds(first, HALF), :] = low[:, :128]
            dout[2 * n + 1, pl.ds(first, HALF), :] = low[:, 128:]
            return 0

        lax.fori_loop(0, 4, tile, 0)

    project(0)
    turn(3)
    arrive(forwards[2])
    arrive(forwards[3])
    project(HALF)

    def level_grads(p, _):
        turned_q = qT[p].astype(F32)
        for e in range(2):
            h = 2 * p + e
            rows = turned_q[e * 64:(e + 1) * 64, :]
            scaled = [
                (lam[LB + 1 + b, pl.ds(h, 1), :] * rows).astype(BF16) for b in range(SEQ_BITS)
            ]
            grads = nn(jnp.concatenate(scaled, axis=0), dout[h]).astype(BF16)
            at = pl.ds(pl.multiple_of(h * 64, 64), 64)
            for b in range(SEQ_BITS):
                lg[b, at, :] = grads[b * 64:(b + 1) * 64, :]
        return 0

    lax.fori_loop(0, PAIRS, level_grads, 0)
    r0 = start([
        remote(lg.at[pl.ds(1, 5), other], rbh, ss, sr, R0, partner),
        remote(lg.at[0], rb0, ss, sr, R0 + 1, partner),
    ])
    arrive(s4)

    def attention(p, _):
        turned_k = kT[p]
        values = vp[p]
        query = qp[p]
        lines = []
        for e in range(2):
            h = 2 * p + e
            mine_q = masked(query, e)
            d = dout[h]
            mine_v = values[:, e * 128:(e + 1) * 128]
            low = (mix_of(h, 0, HALF, 0, ROWS) * nt(mine_v[:HALF], d)).astype(BF16)
            high = (mix_of(h, HALF, HALF, HALF, HALF) * nt(mine_v[HALF:], d[HALF:])).astype(BF16)
            key_low = nn(low, mine_q)
            key_high = nn(high, mine_q[HALF:])
            if e == 0:
                kacc[p, pl.ds(0, HALF), :] = key_low
                kacc[p, pl.ds(HALF, HALF), :] = key_high
            else:
                kacc[p, pl.ds(0, HALF), :] += key_low
                kacc[p, pl.ds(HALF, HALF), :] += key_high
            vacc[p, pl.ds(0, HALF), pl.ds(e * 128, 128)] = nn(sm[h, pl.ds(0, HALF), :], d)
            vacc[p, pl.ds(HALF, HALF), pl.ds(e * 128, 128)] = nn(
                sm[h, pl.ds(HALF, HALF), pl.ds(HALF, HALF)], d[HALF:]
            )
            own_k = turned_k[e * 64:(e + 1) * 64, :]
            line = nn(own_k[:, :HALF], low)
            line_high = nn(own_k[:, HALF:], high)
            at = pl.ds(pl.multiple_of(h * 64, 64), 64)
            states = state_low[:, at, :].reshape(SEQ_BITS * 64, 128)
            read = nt(states, d)
            for b in range(SEQ_BITS):
                line = line + lam[LB + 1 + b, pl.ds(h, 1), :] * read[b * 64:(b + 1) * 64, :]
            lines.append(jnp.concatenate([line[:, :HALF], line[:, HALF:] + line_high], axis=1))
        qo[p] = jnp.concatenate(lines, axis=0).T.astype(BF16)
        return 0

    lax.fori_loop(0, 1, attention, 0)
    arrive(r0)
    rsrc[...] = (lg[pl.ds(1, 5), mine, :].astype(F32) + rbh[...].astype(F32)).astype(BF16)

    def owned(at):
        return pl.ds(pl.multiple_of(at * SLICE, SLICE), SLICE)

    r1 = start([
        remote(rsrc.at[:, owned(flipped(z, i, 3))], rbuf.at[i], ss, sr, R1 + i - 1, z_peer(i))
        for i in range(1, 8)
    ])
    rbuf[0] = rsrc[:, owned(z), :]

    lax.fori_loop(1, 3, attention, 0)
    arrive(r1)
    tops = rbuf[0, pl.ds(3, 2)].astype(F32)
    for i in range(1, 8):
        tops = tops + rbuf[i, pl.ds(3, 2)].astype(F32)
    tsrc[...] = tops.astype(BF16)
    r2 = start([remote(tsrc, tbuf.at[i], ss, sr, R2 + i - 1, x_peer(i)) for i in range(1, 4)])

    lax.fori_loop(3, 4, attention, 0)
    arrive(r2)
    outer = tbuf[1, 0].astype(F32) + tbuf[2, 1].astype(F32) + tbuf[3, 1].astype(F32)
    for r in range(8):
        total = outer
        for i in range(1, 8):
            total = total + rbuf[r ^ i, i.bit_length() - 1].astype(F32)
        rets[r] = total.astype(BF16)
    finals = pl.ds(pl.multiple_of(c * HALF + z * SLICE, SLICE), SLICE)
    r3 = start([remote(rets.at[i], rfin.at[finals], ss, sr, R3 + i - 1, z_peer(i)) for i in range(1, 8)])
    rfin[finals, :] = rets[0]

    outs = []
    for p in range(PAIRS):
        outs.append(pltpu.make_async_copy(qo.at[p], qo_hbm.at[:, pl.ds(p * 128, 128)], out_sem.at[p]))
        outs[-1].start()

    arrive(r3)
    r4 = start([remote(rfin.at[mine], rfin.at[mine], ss, sr, R4, partner)])
    arrive(r4)

    for p in range(PAIRS):
        back = (rfin[pl.ds(p * 128, 128), :].astype(F32) + rb0[pl.ds(p * 128, 128), :].astype(F32)).astype(BF16)
        zero = jnp.zeros((64, 128), BF16)
        spread = jnp.concatenate([
            jnp.concatenate([back[:64], zero], axis=1),
            jnp.concatenate([zero, back[64:]], axis=1),
        ], axis=0)
        ko[p] = (kacc[p] + nt(vp[p], spread)).astype(BF16)
        outs.append(pltpu.make_async_copy(ko.at[p], ko_hbm.at[:, pl.ds(p * 128, 128)], out_sem.at[4 + p]))
        outs[-1].start()
        vo[p] = (vacc[p] + nn(kp[p], spread)).astype(BF16)
        outs.append(pltpu.make_async_copy(vo.at[p], vo_hbm.at[:, pl.ds(p * 256, 256)], out_sem.at[8 + p]))
        outs[-1].start()

    for copy in sent:
        copy.wait_send()
    for copy in outs:
        copy.wait()


def per_device(query_rows, key_rows, value_rows, out_grad, out_weight, level_codes, level_table):
    any_space = pl.BlockSpec(memory_space=pl.ANY)
    vmem = pl.BlockSpec(memory_space=pltpu.VMEM)
    scratch = [
        pltpu.VMEM((PAIRS, ROWS, 128), BF16),
        pltpu.VMEM((PAIRS, ROWS, 128), BF16),
        pltpu.VMEM((PAIRS, ROWS, 256), BF16),
        pltpu.VMEM((4, HEADS * DV, FEAT), BF16),
        pltpu.VMEM((4, ROWS, FEAT), BF16),
        pltpu.VMEM((HEADS, ROWS, DV), BF16),
        pltpu.VMEM((PAIRS, 128, ROWS), BF16),
        pltpu.VMEM((PAIRS, 128, ROWS), BF16),
        pltpu.VMEM((LB + 1 + SEQ_BITS, HEADS, ROWS), F32),
        pltpu.VMEM((ROWS // BLK, HEADS, ROWS), F32),
        pltpu.VMEM((HEADS, ROWS, ROWS), BF16),
        pltpu.VMEM((ROWS, 128), F32),
        pltpu.VMEM((ROWS, 128), F32),
        pltpu.VMEM((8, HALF, 128), BF16),
        pltpu.VMEM((4, HALF, 128), BF16),
        pltpu.VMEM((SEQ_BITS, ROWS, 128), BF16),
        pltpu.VMEM((SEQ_BITS, ROWS, 128), BF16),
        pltpu.VMEM((ROWS, 128), BF16),
        pltpu.VMEM((5, HALF, 128), BF16),
        pltpu.VMEM((5, HALF, 128), BF16),
        pltpu.VMEM((8, 5, SLICE, 128), BF16),
        pltpu.VMEM((2, SLICE, 128), BF16),
        pltpu.VMEM((4, 2, SLICE, 128), BF16),
        pltpu.VMEM((8, SLICE, 128), BF16),
        pltpu.VMEM((ROWS, 128), BF16),
        pltpu.VMEM((PAIRS, ROWS, 128), F32),
        pltpu.VMEM((PAIRS, ROWS, 256), F32),
        pltpu.VMEM((PAIRS, ROWS, 128), BF16),
        pltpu.VMEM((PAIRS, ROWS, 128), BF16),
        pltpu.VMEM((PAIRS, ROWS, 256), BF16),
        pltpu.SemaphoreType.DMA((17,)),
        pltpu.SemaphoreType.DMA((12,)),
        pltpu.SemaphoreType.DMA((16,)),
        pltpu.SemaphoreType.DMA((16,)),
        pltpu.SemaphoreType.DMA((N_SEM,)),
        pltpu.SemaphoreType.DMA((N_SEM,)),
    ]
    return pl.pallas_call(
        kernel,
        out_shape=(
            jax.ShapeDtypeStruct((ROWS, HEADS * DK), BF16),
            jax.ShapeDtypeStruct((ROWS, HEADS * DK), BF16),
            jax.ShapeDtypeStruct((ROWS, HEADS * DV), BF16),
        ),
        in_specs=[any_space] * 5 + [vmem] * 2,
        out_specs=(any_space,) * 3,
        scratch_shapes=scratch,
        compiler_params=pltpu.CompilerParams(
            collective_id=0, has_side_effects=True, vmem_limit_bytes=56 * 1024 * 1024
        ),
        cost_estimate=pl.CostEstimate(flops=8_000_000_000, bytes_accessed=12_000_000, transcendentals=0),
    )(query_rows, key_rows, value_rows, out_grad, out_weight, level_codes, level_table)


def solution(mesh):
    return jax.shard_map(
        per_device,
        mesh=mesh,
        in_specs=(
            P("seq", "head"),
            P("seq", "head"),
            P("seq", "head"),
            P("seq", "head"),
            P("head", None),
            P(None, "head", "seq"),
            P("head", None),
        ),
        out_specs=(P("seq", "head"), P("seq", "head"), P("seq", "head")),
        check_vma=False,
    )
```

```python
import jax
import jax.numpy as jnp
from jax import lax
from jax.experimental import pallas as pl
from jax.experimental.pallas import tpu as pltpu
from jax.sharding import PartitionSpec as P

DK = 64
DV = 128
BLK = 64
LB = 3
SEQ_BITS = 6
ROWS = 512
HEADS = 8
PAIRS = 4
FEAT = 768
CHUNKS = 4
CROWS = ROWS // CHUNKS
HALF = 256
SLICE = 32
SCALES = [float((DK * BLK * 2 ** max(level - 1, 0)) ** -0.5) for level in range(LB + 1 + SEQ_BITS)]

F32 = jnp.float32
BF16 = jnp.bfloat16

S0, S1, S2, S4, R0, R1, R2, R3, R4, N_SEM = 0, 1, 8, 11, 16, 27, 41, 44, 51, 52


def nt(a, b):
    return lax.dot_general(a, b, (((1,), (1,)), ((), ())), preferred_element_type=F32)


def nn(a, b):
    return lax.dot_general(a, b, (((1,), (0,)), ((), ())), preferred_element_type=F32)


def flipped(value, mask, bits):
    out = value
    for k in range(bits):
        if mask >> k & 1:
            out = out + (1 - 2 * ((value // 2**k) % 2)) * 2**k
    return out


def kernel(
    q_hbm, k_hbm, v_hbm, og_hbm, w_hbm, codes_ref, table_ref,
    qo_hbm, ko_hbm, vo_hbm, ret_ref,
    qp, kp, vp, w4, gath, dout, kT, qT, lam, inner, sm,
    gsb, pgs, zbuf, xbuf, state_low,
    lg, rb0, rbh, rsrc, rbuf, tsrc, tbuf, rets, rfin,
    kacc, vacc, qo, pacc, lgacc,
    loc_sem, out_sem, ys, yr, ss, sr,
):
    g = lax.axis_index("seq")
    y = lax.axis_index("head")
    c = g % 2
    z = (g // 2) % 8
    x = g // 16
    right, left, across = (y + 1) % 4, (y + 3) % 4, (y + 2) % 4

    def z_peer(i):
        return (x * 16 + flipped(z, i, 3) * 2 + c, y)

    def x_peer(i):
        return (flipped(x, i, 2) * 16 + z * 2 + c, y)

    partner = (g + 1 - 2 * c, y)
    peers = [partner, (g, right), (g, left)]
    peers += [z_peer(i) for i in range(1, 8)] + [x_peer(i) for i in range(1, 4)]

    loads = []
    for p in range(PAIRS):
        loads.append(pltpu.make_async_copy(k_hbm.at[:, pl.ds(p * 128, 128)], kp.at[p], loc_sem.at[len(loads)]))
    for p in range(PAIRS):
        loads.append(pltpu.make_async_copy(v_hbm.at[:, pl.ds(p * 256, 256)], vp.at[p], loc_sem.at[len(loads)]))
    for p in range(PAIRS):
        loads.append(pltpu.make_async_copy(q_hbm.at[:, pl.ds(p * 128, 128)], qp.at[p], loc_sem.at[len(loads)]))
    loads.append(pltpu.make_async_copy(og_hbm, gath.at[y], loc_sem.at[len(loads)]))
    for p in range(4):
        loads.append(pltpu.make_async_copy(w_hbm.at[:, pl.ds(p * FEAT, FEAT)], w4.at[p], loc_sem.at[len(loads)]))
    for load in loads:
        load.start()

    barrier = pltpu.get_barrier_semaphore()
    for peer in peers:
        pl.semaphore_signal(barrier, inc=1, device_id=peer, device_id_type=pl.DeviceIdType.MESH)

    for load in loads[:8]:
        load.wait()

    def states_of(p, _):
        kT[p] = kp[p].T
        both = nn(kT[p], vp[p])
        at = pl.multiple_of(p * 128, 128)
        gsb[pl.ds(at, 64), :] = both[:64, :128]
        gsb[pl.ds(at + 64, 64), :] = both[64:, 128:]
        return 0

    lax.fori_loop(0, PAIRS, states_of, 0)
    pl.semaphore_wait(barrier, len(peers))

    def remote(src, dst, send, recv, slot, to):
        return pltpu.make_async_remote_copy(
            src_ref=src, dst_ref=dst, send_sem=send.at[slot], recv_sem=recv.at[slot],
            device_id=to, device_id_type=pl.DeviceIdType.MESH,
        )

    def own(j):
        rows = pl.ds(j * CROWS, CROWS)
        return [
            remote(og_hbm.at[rows], gath.at[y, rows], ys, yr, j, (g, right)),
            remote(og_hbm.at[rows], gath.at[y, rows], ys, yr, 4 + j, (g, left)),
        ]

    def forward(j):
        first = pl.ds(j * CROWS, CROWS // 2)
        second = pl.ds(j * CROWS + CROWS // 2, CROWS // 2)
        return [
            remote(gath.at[left, first], gath.at[left, first], ys, yr, 8 + j, (g, right)),
            remote(gath.at[right, second], gath.at[right, second], ys, yr, 12 + j, (g, left)),
        ]

    def start(copies):
        for copy in copies:
            copy.start()
        sent.extend(copies)
        return copies

    def arrive(copies):
        for copy in copies:
            copy.wait_recv()

    sent = []
    owns = [own(j) for j in range(CHUNKS)]
    forwards = [forward(j) for j in range(CHUNKS)]
    for j in range(CHUNKS):
        start(owns[j])
    s0 = start([remote(gsb, pgs, ss, sr, S0, partner)])

    table = table_ref[...]
    columns = [jnp.broadcast_to(table[:, j:j + 1], (HEADS, ROWS)) for j in range(16)]
    for level in range(LB + 1 + SEQ_BITS):
        codes = codes_ref[level]
        looked = jnp.zeros((HEADS, ROWS), F32)
        for j in range(16):
            looked = jnp.where(codes == j, columns[j], looked)
        looked = looked * SCALES[level]
        if level > LB:
            looked = looked * ((g // 2 ** (level - LB - 1)) % 2).astype(F32)
        lam[level] = looked
    token_block = lax.broadcasted_iota(jnp.int32, (HEADS, ROWS), 1) // BLK
    for cs in range(ROWS // BLK):
        line = jnp.zeros((HEADS, ROWS), F32)
        for ct in range(cs, ROWS // BLK):
            line = jnp.where(token_block == ct, lam[(ct ^ cs).bit_length()], line)
        inner[cs] = line

    for load in loads[8:12]:
        load.wait()

    def turned(p, _):
        qT[p] = qp[p].T
        return 0

    lax.fori_loop(0, PAIRS, turned, 0)

    mine = pl.ds(pl.multiple_of(c * HALF, HALF), HALF)
    other = pl.ds(pl.multiple_of((1 - c) * HALF, HALF), HALF)
    arrive(s0)
    zbuf[0] = (gsb[mine, :] + pgs[mine, :]).astype(BF16)
    s1 = start([remote(zbuf.at[0], zbuf.at[i], ss, sr, S1 + i - 1, z_peer(i)) for i in range(1, 8)])
    state_low[0] = pgs[...].astype(BF16)

    def turn(j):
        arrive(owns[j])
        start(forwards[j])

    def mix_of(h, s0_, count, t0_, width):
        lines = [
            jnp.broadcast_to(inner[s0_ // BLK + i, pl.ds(h, 1), pl.ds(t0_, width)], (BLK, width))
            for i in range(count // BLK)
        ]
        mix = jnp.concatenate(lines, axis=0)
        s_at = lax.broadcasted_iota(jnp.int32, (count, width), 0) + s0_
        t_at = lax.broadcasted_iota(jnp.int32, (count, width), 1) + t0_
        return jnp.where(s_at <= t_at, mix, 0.0)

    def masked(pair, e):
        lane = lax.broadcasted_iota(jnp.int32, pair.shape, 1)
        return jnp.where((lane >= 64) == (e == 1), pair, jnp.zeros_like(pair))

    def scores_of(p, _):
        for e in range(2):
            h = 2 * p + e
            keys = masked(kp[p], e)
            query = qp[p]
            sm[h, pl.ds(0, HALF), :] = (mix_of(h, 0, HALF, 0, ROWS) * nt(keys[:HALF], query)).astype(BF16)
            sm[h, pl.ds(HALF, HALF), pl.ds(HALF, HALF)] = (
                mix_of(h, HALF, HALF, HALF, HALF) * nt(keys[HALF:], query[HALF:])
            ).astype(BF16)
        return 0

    lax.fori_loop(0, PAIRS, scores_of, 0)

    def project(slots, first, count, begin, end):
        def tile(n, _):
            cols = pl.ds(pl.multiple_of(n * 256, 256), 256)
            rows = pl.ds(first, count)
            total = None if begin else pacc[n, rows, :]
            for d in slots:
                part = nt(gath[d, rows, :], w4[d, cols, :])
                total = part if total is None else total + part
            if end:
                low = total.astype(BF16)
                dout[2 * n, rows, :] = low[:, :128]
                dout[2 * n + 1, rows, :] = low[:, 128:]
            else:
                pacc[n, rows, :] = total
            return 0

        lax.fori_loop(0, 4, tile, 0)

    def level_part(p, e, first):
        h = 2 * p + e
        rows = qT[p, e * 64:(e + 1) * 64, first:first + HALF].astype(F32)
        scaled = [
            (lam[LB + 1 + b, pl.ds(h, 1), first:first + HALF] * rows).astype(BF16) for b in range(SEQ_BITS)
        ]
        return nn(jnp.concatenate(scaled, axis=0), dout[h, first:first + HALF, :])

    def level_first(p, _):
        for e in range(2):
            lgacc[p, e] = level_part(p, e, 0)
        return 0

    def level_rest(p, _):
        for e in range(2):
            grads = (lgacc[p, e] + level_part(p, e, HALF)).astype(BF16)
            at = pl.ds(pl.multiple_of(p * 128 + e * 64, 64), 64)
            for b in range(SEQ_BITS):
                lg[b, at, :] = grads[b * 64:(b + 1) * 64, :]
        return 0

    for load in loads[12:]:
        load.wait()
    project([y], 0, ROWS, True, False)
    turn(0)
    turn(1)
    project([left, right], 0, HALF, False, False)
    turn(2)
    turn(3)

    arrive(s1)
    parts = [zbuf[i].astype(F32) for i in range(8)]
    pair1 = parts[2] + parts[3]
    quad = (parts[4] + parts[5]) + (parts[6] + parts[7])
    xbuf[0] = ((parts[0] + parts[1]) + pair1 + quad).astype(BF16)
    s2 = start([remote(xbuf.at[0], xbuf.at[i], ss, sr, S2 + i - 1, x_peer(i)) for i in range(1, 4)])
    state_low[1, mine, :] = zbuf[1]
    state_low[2, mine, :] = pair1.astype(BF16)
    state_low[3, mine, :] = quad.astype(BF16)

    project([left, right], HALF, HALF, False, False)
    arrive(forwards[0])
    arrive(forwards[1])
    project([across], 0, HALF, False, True)
    lax.fori_loop(0, PAIRS, level_first, 0)

    arrive(s2)
    state_low[4, mine, :] = xbuf[1]
    state_low[5, mine, :] = (xbuf[2].astype(F32) + xbuf[3].astype(F32)).astype(BF16)
    s4 = start([
        remote(state_low.at[b, mine], state_low.at[b, mine], ss, sr, S4 + b - 1, partner) for b in range(1, SEQ_BITS)
    ])

    arrive(forwards[2])
    arrive(forwards[3])
    project([across], HALF, HALF, False, True)

    r0 = []
    for i in range(2):
        p = 2 * (1 - c) + i
        level_rest(p, 0)
        rows = pl.ds(pl.multiple_of(p * 128, 128), 128)
        r0 += start([
            remote(lg.at[1 + b, rows], rbh.at[b, pl.ds(i * 128, 128)], ss, sr, R0 + 5 * i + b, partner)
            for b in range(5)
        ])
    for i in range(2):
        level_rest(2 * c + i, 0)
    arrive(r0)
    rsrc[...] = (lg[pl.ds(1, 5), mine, :].astype(F32) + rbh[...].astype(F32)).astype(BF16)

    def owned(at):
        return pl.ds(pl.multiple_of(at * SLICE, SLICE), SLICE)

    r1x = start([
        remote(rsrc.at[pl.ds(3, 2), owned(flipped(z, i, 3))], rbuf.at[i, pl.ds(3, 2)], ss, sr, R1 + i - 1, z_peer(i))
        for i in range(1, 8)
    ])
    r1 = start([
        remote(rsrc.at[pl.ds(0, 3), owned(flipped(z, i, 3))], rbuf.at[i, pl.ds(0, 3)], ss, sr, R1 + 6 + i, z_peer(i))
        for i in range(1, 8)
    ])
    rbuf[0] = rsrc[:, owned(z), :]
    rb = start([remote(lg.at[0], rb0, ss, sr, R0 + 10, partner)])
    arrive(s4)

    def attention(p, _):
        turned_k = kT[p]
        values = vp[p]
        query = qp[p]
        lines = []
        for e in range(2):
            h = 2 * p + e
            mine_q = masked(query, e)
            d = dout[h]
            mine_v = values[:, e * 128:(e + 1) * 128]
            low = (mix_of(h, 0, HALF, 0, ROWS) * nt(mine_v[:HALF], d)).astype(BF16)
            high = (mix_of(h, HALF, HALF, HALF, HALF) * nt(mine_v[HALF:], d[HALF:])).astype(BF16)
            key_low = nn(low, mine_q)
            key_high = nn(high, mine_q[HALF:])
            if e == 0:
                kacc[p, pl.ds(0, HALF), :] = key_low
                kacc[p, pl.ds(HALF, HALF), :] = key_high
            else:
                kacc[p, pl.ds(0, HALF), :] += key_low
                kacc[p, pl.ds(HALF, HALF), :] += key_high
            vacc[p, pl.ds(0, HALF), pl.ds(e * 128, 128)] = nn(sm[h, pl.ds(0, HALF), :], d)
            vacc[p, pl.ds(HALF, HALF), pl.ds(e * 128, 128)] = nn(
                sm[h, pl.ds(HALF, HALF), pl.ds(HALF, HALF)], d[HALF:]
            )
            own_k = turned_k[e * 64:(e + 1) * 64, :]
            line = nn(own_k[:, :HALF], low)
            line_high = nn(own_k[:, HALF:], high)
            at = pl.ds(pl.multiple_of(h * 64, 64), 64)
            states = state_low[:, at, :].reshape(SEQ_BITS * 64, 128)
            read = nt(states, d)
            for b in range(SEQ_BITS):
                line = line + lam[LB + 1 + b, pl.ds(h, 1), :] * read[b * 64:(b + 1) * 64, :]
            lines.append(jnp.concatenate([line[:, :HALF], line[:, HALF:] + line_high], axis=1))
        qo[p] = jnp.concatenate(lines, axis=0).T.astype(BF16)
        return 0

    def store(p):
        copies = [
            pltpu.make_async_copy(qo.at[p], qo_hbm.at[p], out_sem.at[p]),
            pltpu.make_async_copy(kacc.at[p], ko_hbm.at[p], out_sem.at[4 + p]),
            pltpu.make_async_copy(vacc.at[p], vo_hbm.at[p], out_sem.at[8 + p]),
        ]
        for copy in copies:
            copy.start()
        outs.extend(copies)

    outs = []

    lax.fori_loop(0, 2, attention, 0)
    store(0)
    store(1)
    arrive(r1x)
    tops = rbuf[0, pl.ds(3, 2)].astype(F32)
    for i in range(1, 8):
        tops = tops + rbuf[i, pl.ds(3, 2)].astype(F32)
    tsrc[...] = tops.astype(BF16)
    r2 = start([remote(tsrc, tbuf.at[i], ss, sr, R2 + i - 1, x_peer(i)) for i in range(1, 4)])

    lax.fori_loop(2, 4, attention, 0)
    store(2)
    store(3)
    arrive(r1)
    arrive(r2)
    outer = tbuf[1, 0].astype(F32) + tbuf[2, 1].astype(F32) + tbuf[3, 1].astype(F32)
    for r in range(8):
        total = outer
        for i in range(1, 8):
            total = total + rbuf[r ^ i, i.bit_length() - 1].astype(F32)
        rets[r] = total.astype(BF16)
    finals = pl.ds(pl.multiple_of(c * HALF + z * SLICE, SLICE), SLICE)
    r3 = start([remote(rets.at[i], rfin.at[finals], ss, sr, R3 + i - 1, z_peer(i)) for i in range(1, 8)])
    rfin[finals, :] = rets[0]
    arrive(rb)
    arrive(r3)
    r4 = start([remote(rfin.at[mine], rfin.at[mine], ss, sr, R4, partner)])
    for copy in outs:
        copy.wait()
    arrive(r4)
    ret_ref[...] = (rfin[...].astype(F32) + rb0[...].astype(F32)).astype(BF16)
    for copy in sent:
        copy.wait_send()


def finish(ret_ref, k_ref, v_ref, q_ref, kacc_ref, vacc_ref, qo_ref, ko_ref, vo_ref):
    back = ret_ref[...]
    zero = jnp.zeros((64, 128), BF16)
    spread = jnp.concatenate([
        jnp.concatenate([back[:64], zero], axis=1),
        jnp.concatenate([zero, back[64:]], axis=1),
    ], axis=0)
    qo_ref[...] = q_ref[0]
    ko_ref[...] = (kacc_ref[0] + nt(v_ref[...], spread)).astype(BF16)
    vo_ref[...] = (vacc_ref[0] + nn(k_ref[...], spread)).astype(BF16)


def per_device(query_rows, key_rows, value_rows, out_grad, out_weight, level_codes, level_table):
    any_space = pl.BlockSpec(memory_space=pl.ANY)
    vmem = pl.BlockSpec(memory_space=pltpu.VMEM)
    scratch = [
        pltpu.VMEM((PAIRS, ROWS, 128), BF16),
        pltpu.VMEM((PAIRS, ROWS, 128), BF16),
        pltpu.VMEM((PAIRS, ROWS, 256), BF16),
        pltpu.VMEM((4, HEADS * DV, FEAT), BF16),
        pltpu.VMEM((4, ROWS, FEAT), BF16),
        pltpu.VMEM((HEADS, ROWS, DV), BF16),
        pltpu.VMEM((PAIRS, 128, ROWS), BF16),
        pltpu.VMEM((PAIRS, 128, ROWS), BF16),
        pltpu.VMEM((LB + 1 + SEQ_BITS, HEADS, ROWS), F32),
        pltpu.VMEM((ROWS // BLK, HEADS, ROWS), F32),
        pltpu.VMEM((HEADS, ROWS, ROWS), BF16),
        pltpu.VMEM((ROWS, 128), F32),
        pltpu.VMEM((ROWS, 128), F32),
        pltpu.VMEM((8, HALF, 128), BF16),
        pltpu.VMEM((4, HALF, 128), BF16),
        pltpu.VMEM((SEQ_BITS, ROWS, 128), BF16),
        pltpu.VMEM((SEQ_BITS, ROWS, 128), BF16),
        pltpu.VMEM((ROWS, 128), BF16),
        pltpu.VMEM((5, HALF, 128), BF16),
        pltpu.VMEM((5, HALF, 128), BF16),
        pltpu.VMEM((8, 5, SLICE, 128), BF16),
        pltpu.VMEM((2, SLICE, 128), BF16),
        pltpu.VMEM((4, 2, SLICE, 128), BF16),
        pltpu.VMEM((8, SLICE, 128), BF16),
        pltpu.VMEM((ROWS, 128), BF16),
        pltpu.VMEM((PAIRS, ROWS, 128), F32),
        pltpu.VMEM((PAIRS, ROWS, 256), F32),
        pltpu.VMEM((PAIRS, ROWS, 128), BF16),
        pltpu.VMEM((4, ROWS, 256), F32),
        pltpu.VMEM((PAIRS, 2, SEQ_BITS * 64, 128), F32),
        pltpu.SemaphoreType.DMA((17,)),
        pltpu.SemaphoreType.DMA((12,)),
        pltpu.SemaphoreType.DMA((16,)),
        pltpu.SemaphoreType.DMA((16,)),
        pltpu.SemaphoreType.DMA((N_SEM,)),
        pltpu.SemaphoreType.DMA((N_SEM,)),
    ]
    queries, keys, values, returned = pl.pallas_call(
        kernel,
        out_shape=(
            jax.ShapeDtypeStruct((PAIRS, ROWS, 128), BF16),
            jax.ShapeDtypeStruct((PAIRS, ROWS, 128), F32),
            jax.ShapeDtypeStruct((PAIRS, ROWS, 256), F32),
            jax.ShapeDtypeStruct((ROWS, 128), BF16),
        ),
        in_specs=[any_space] * 5 + [vmem] * 2,
        out_specs=(any_space,) * 3 + (vmem,),
        scratch_shapes=scratch,
        compiler_params=pltpu.CompilerParams(
            collective_id=0, has_side_effects=True, vmem_limit_bytes=56 * 1024 * 1024
        ),
        cost_estimate=pl.CostEstimate(flops=8_000_000_000, bytes_accessed=12_000_000, transcendentals=0),
    )(query_rows, key_rows, value_rows, out_grad, out_weight, level_codes, level_table)
    narrow = pl.BlockSpec((ROWS, 128), lambda p: (0, p))
    wide = pl.BlockSpec((ROWS, 256), lambda p: (0, p))
    narrow_pair = pl.BlockSpec((1, ROWS, 128), lambda p: (p, 0, 0))
    wide_pair = pl.BlockSpec((1, ROWS, 256), lambda p: (p, 0, 0))
    return pl.pallas_call(
        finish,
        grid=(PAIRS,),
        out_shape=(
            jax.ShapeDtypeStruct((ROWS, HEADS * DK), BF16),
            jax.ShapeDtypeStruct((ROWS, HEADS * DK), BF16),
            jax.ShapeDtypeStruct((ROWS, HEADS * DV), BF16),
        ),
        in_specs=[pl.BlockSpec((128, 128), lambda p: (p, 0)), narrow, wide, narrow_pair, narrow_pair, wide_pair],
        out_specs=(narrow, narrow, wide),
        cost_estimate=pl.CostEstimate(flops=500_000_000, bytes_accessed=8_000_000, transcendentals=0),
    )(returned, key_rows, value_rows, queries, keys, values)


def solution(mesh):
    return jax.shard_map(
        per_device,
        mesh=mesh,
        in_specs=(
            P("seq", "head"),
            P("seq", "head"),
            P("seq", "head"),
            P("seq", "head"),
            P("head", None),
            P(None, "head", "seq"),
            P("head", None),
        ),
        out_specs=(P("seq", "head"), P("seq", "head"), P("seq", "head")),
        check_vma=False,
    )
```

```python
import jax
import jax.numpy as jnp
from jax import lax
from jax.experimental import pallas as pl
from jax.experimental.pallas import tpu as pltpu
from jax.sharding import PartitionSpec as P

DK = 64
DV = 128
BLK = 64
LB = 3
SEQ_BITS = 6
ROWS = 512
HEADS = 8
PAIRS = 4
FEAT = 768
CHUNKS = 4
CROWS = ROWS // CHUNKS
HALF = 256
SLICE = 32
SCALES = [float((DK * BLK * 2 ** max(level - 1, 0)) ** -0.5) for level in range(LB + 1 + SEQ_BITS)]

F32 = jnp.float32
BF16 = jnp.bfloat16

S0, S1, S2, S4, R0, R1, R2, R3, R4, N_SEM = 0, 1, 8, 11, 16, 27, 41, 44, 51, 52


def nt(a, b):
    return lax.dot_general(a, b, (((1,), (1,)), ((), ())), preferred_element_type=F32)


def nn(a, b):
    return lax.dot_general(a, b, (((1,), (0,)), ((), ())), preferred_element_type=F32)


def flipped(value, mask, bits):
    out = value
    for k in range(bits):
        if mask >> k & 1:
            out = out + (1 - 2 * ((value // 2**k) % 2)) * 2**k
    return out


def kernel(
    q_hbm, k_hbm, v_hbm, og_hbm, w_hbm, codes_hbm, table_hbm,
    qo, kacc, vacc, ret_ref, kp, vp,
    qp, w4, gath, dout, kT, qT, lam, inner, sm,
    gsb, pgs, zbuf, xbuf, state_low,
    lg, rb0, rbh, rsrc, rbuf, tsrc, tbuf, rets, rfin,
    pacc, lgacc, codes_ref, table_ref,
    loc_sem, ys, yr, ss, sr,
):
    g = lax.axis_index("seq")
    y = lax.axis_index("head")
    c = g % 2
    z = (g // 2) % 8
    x = g // 16
    right, left, across = (y + 1) % 4, (y + 3) % 4, (y + 2) % 4

    def z_peer(i):
        return (x * 16 + flipped(z, i, 3) * 2 + c, y)

    def x_peer(i):
        return (flipped(x, i, 2) * 16 + z * 2 + c, y)

    partner = (g + 1 - 2 * c, y)
    peers = [partner, (g, right), (g, left)]
    peers += [z_peer(i) for i in range(1, 8)] + [x_peer(i) for i in range(1, 4)]

    loads = []
    for p in range(PAIRS):
        loads.append(pltpu.make_async_copy(k_hbm.at[:, pl.ds(p * 128, 128)], kp.at[p], loc_sem.at[len(loads)]))
    for p in range(PAIRS):
        loads.append(pltpu.make_async_copy(v_hbm.at[:, pl.ds(p * 256, 256)], vp.at[p], loc_sem.at[len(loads)]))
    for p in range(PAIRS):
        loads.append(pltpu.make_async_copy(q_hbm.at[:, pl.ds(p * 128, 128)], qp.at[p], loc_sem.at[len(loads)]))
    loads.append(pltpu.make_async_copy(codes_hbm, codes_ref, loc_sem.at[len(loads)]))
    loads.append(pltpu.make_async_copy(table_hbm, table_ref, loc_sem.at[len(loads)]))
    loads.append(pltpu.make_async_copy(og_hbm, gath.at[y], loc_sem.at[len(loads)]))
    for p in range(4):
        loads.append(pltpu.make_async_copy(w_hbm.at[:, pl.ds(p * FEAT, FEAT)], w4.at[p], loc_sem.at[len(loads)]))
    for load in loads:
        load.start()

    barrier = pltpu.get_barrier_semaphore()
    for peer in peers:
        pl.semaphore_signal(barrier, inc=1, device_id=peer, device_id_type=pl.DeviceIdType.MESH)

    for load in loads[:8]:
        load.wait()

    def states_of(p, _):
        kT[p] = kp[p].T
        both = nn(kT[p], vp[p])
        at = pl.multiple_of(p * 128, 128)
        gsb[pl.ds(at, 64), :] = both[:64, :128]
        gsb[pl.ds(at + 64, 64), :] = both[64:, 128:]
        return 0

    lax.fori_loop(0, PAIRS, states_of, 0)
    pl.semaphore_wait(barrier, len(peers))

    def remote(src, dst, send, recv, slot, to):
        return pltpu.make_async_remote_copy(
            src_ref=src, dst_ref=dst, send_sem=send.at[slot], recv_sem=recv.at[slot],
            device_id=to, device_id_type=pl.DeviceIdType.MESH,
        )

    def own(j):
        rows = pl.ds(j * CROWS, CROWS)
        return [
            remote(og_hbm.at[rows], gath.at[y, rows], ys, yr, j, (g, right)),
            remote(og_hbm.at[rows], gath.at[y, rows], ys, yr, 4 + j, (g, left)),
        ]

    def forward(j):
        first = pl.ds(j * CROWS, CROWS // 2)
        second = pl.ds(j * CROWS + CROWS // 2, CROWS // 2)
        return [
            remote(gath.at[left, first], gath.at[left, first], ys, yr, 8 + j, (g, right)),
            remote(gath.at[right, second], gath.at[right, second], ys, yr, 12 + j, (g, left)),
        ]

    def start(copies):
        for copy in copies:
            copy.start()
        sent.extend(copies)
        return copies

    def arrive(copies):
        for copy in copies:
            copy.wait_recv()

    sent = []
    owns = [own(j) for j in range(CHUNKS)]
    forwards = [forward(j) for j in range(CHUNKS)]
    for j in range(CHUNKS):
        start(owns[j])
    s0 = start([remote(gsb, pgs, ss, sr, S0, partner)])

    for load in loads[8:14]:
        load.wait()
    table = table_ref[...]
    columns = [jnp.broadcast_to(table[:, j:j + 1], (HEADS, ROWS)) for j in range(16)]
    for level in range(LB + 1 + SEQ_BITS):
        codes = codes_ref[level]
        looked = jnp.zeros((HEADS, ROWS), F32)
        for j in range(16):
            looked = jnp.where(codes == j, columns[j], looked)
        looked = looked * SCALES[level]
        if level > LB:
            looked = looked * ((g // 2 ** (level - LB - 1)) % 2).astype(F32)
        lam[level] = looked
    token_block = lax.broadcasted_iota(jnp.int32, (HEADS, ROWS), 1) // BLK
    for cs in range(ROWS // BLK):
        line = jnp.zeros((HEADS, ROWS), F32)
        for ct in range(cs, ROWS // BLK):
            line = jnp.where(token_block == ct, lam[(ct ^ cs).bit_length()], line)
        inner[cs] = line

    def turned(p, _):
        qT[p] = qp[p].T
        return 0

    lax.fori_loop(0, PAIRS, turned, 0)

    mine = pl.ds(pl.multiple_of(c * HALF, HALF), HALF)
    other = pl.ds(pl.multiple_of((1 - c) * HALF, HALF), HALF)
    arrive(s0)
    zbuf[0] = (gsb[mine, :] + pgs[mine, :]).astype(BF16)
    s1 = start([remote(zbuf.at[0], zbuf.at[i], ss, sr, S1 + i - 1, z_peer(i)) for i in range(1, 8)])
    state_low[0] = pgs[...].astype(BF16)

    def turn(j):
        arrive(owns[j])
        start(forwards[j])

    def mix_of(h, s0_, count, t0_, width):
        lines = [
            jnp.broadcast_to(inner[s0_ // BLK + i, pl.ds(h, 1), pl.ds(t0_, width)], (BLK, width))
            for i in range(count // BLK)
        ]
        mix = jnp.concatenate(lines, axis=0)
        s_at = lax.broadcasted_iota(jnp.int32, (count, width), 0) + s0_
        t_at = lax.broadcasted_iota(jnp.int32, (count, width), 1) + t0_
        return jnp.where(s_at <= t_at, mix, 0.0)

    def masked(pair, e):
        lane = lax.broadcasted_iota(jnp.int32, pair.shape, 1)
        return jnp.where((lane >= 64) == (e == 1), pair, jnp.zeros_like(pair))

    def scores_of(p, _):
        for e in range(2):
            h = 2 * p + e
            keys = masked(kp[p], e)
            query = qp[p]
            sm[h, pl.ds(0, HALF), :] = (mix_of(h, 0, HALF, 0, ROWS) * nt(keys[:HALF], query)).astype(BF16)
            sm[h, pl.ds(HALF, HALF), pl.ds(HALF, HALF)] = (
                mix_of(h, HALF, HALF, HALF, HALF) * nt(keys[HALF:], query[HALF:])
            ).astype(BF16)
        return 0

    lax.fori_loop(0, PAIRS, scores_of, 0)

    def project(slots, first, count, begin, end):
        def tile(n, _):
            cols = pl.ds(pl.multiple_of(n * 256, 256), 256)
            rows = pl.ds(first, count)
            total = None if begin else pacc[n, rows, :]
            for d in slots:
                part = nt(gath[d, rows, :], w4[d, cols, :])
                total = part if total is None else total + part
            if end:
                low = total.astype(BF16)
                dout[2 * n, rows, :] = low[:, :128]
                dout[2 * n + 1, rows, :] = low[:, 128:]
            else:
                pacc[n, rows, :] = total
            return 0

        lax.fori_loop(0, 4, tile, 0)

    def level_part(p, e, first):
        h = 2 * p + e
        rows = qT[p, e * 64:(e + 1) * 64, first:first + HALF].astype(F32)
        scaled = [
            (lam[LB + 1 + b, pl.ds(h, 1), first:first + HALF] * rows).astype(BF16) for b in range(SEQ_BITS)
        ]
        return nn(jnp.concatenate(scaled, axis=0), dout[h, first:first + HALF, :])

    def level_first(p, _):
        for e in range(2):
            lgacc[p, e] = level_part(p, e, 0)
        return 0

    def level_rest(p, _):
        for e in range(2):
            grads = (lgacc[p, e] + level_part(p, e, HALF)).astype(BF16)
            at = pl.ds(pl.multiple_of(p * 128 + e * 64, 64), 64)
            for b in range(SEQ_BITS):
                lg[b, at, :] = grads[b * 64:(b + 1) * 64, :]
        return 0

    for load in loads[14:]:
        load.wait()
    project([y], 0, ROWS, True, False)
    turn(0)
    turn(1)
    project([left, right], 0, HALF, False, False)
    turn(2)
    turn(3)

    arrive(s1)
    parts = [zbuf[i].astype(F32) for i in range(8)]
    pair1 = parts[2] + parts[3]
    quad = (parts[4] + parts[5]) + (parts[6] + parts[7])
    xbuf[0] = ((parts[0] + parts[1]) + pair1 + quad).astype(BF16)
    s2 = start([remote(xbuf.at[0], xbuf.at[i], ss, sr, S2 + i - 1, x_peer(i)) for i in range(1, 4)])
    state_low[1, mine, :] = zbuf[1]
    state_low[2, mine, :] = pair1.astype(BF16)
    state_low[3, mine, :] = quad.astype(BF16)

    project([left, right], HALF, HALF, False, False)
    arrive(forwards[0])
    arrive(forwards[1])
    project([across], 0, HALF, False, True)
    lax.fori_loop(0, PAIRS, level_first, 0)

    arrive(s2)
    state_low[4, mine, :] = xbuf[1]
    state_low[5, mine, :] = (xbuf[2].astype(F32) + xbuf[3].astype(F32)).astype(BF16)
    s4 = start([
        remote(state_low.at[b, mine], state_low.at[b, mine], ss, sr, S4 + b - 1, partner) for b in range(1, SEQ_BITS)
    ])

    arrive(forwards[2])
    arrive(forwards[3])
    project([across], HALF, HALF, False, True)

    r0 = []
    for i in range(2):
        p = 2 * (1 - c) + i
        level_rest(p, 0)
        rows = pl.ds(pl.multiple_of(p * 128, 128), 128)
        r0 += start([
            remote(lg.at[1 + b, rows], rbh.at[b, pl.ds(i * 128, 128)], ss, sr, R0 + 5 * i + b, partner)
            for b in range(5)
        ])
    for i in range(2):
        level_rest(2 * c + i, 0)
    arrive(r0)
    rsrc[...] = (lg[pl.ds(1, 5), mine, :].astype(F32) + rbh[...].astype(F32)).astype(BF16)

    def owned(at):
        return pl.ds(pl.multiple_of(at * SLICE, SLICE), SLICE)

    r1x = start([
        remote(rsrc.at[pl.ds(3, 2), owned(flipped(z, i, 3))], rbuf.at[i, pl.ds(3, 2)], ss, sr, R1 + i - 1, z_peer(i))
        for i in range(1, 8)
    ])
    r1 = start([
        remote(rsrc.at[pl.ds(0, 3), owned(flipped(z, i, 3))], rbuf.at[i, pl.ds(0, 3)], ss, sr, R1 + 6 + i, z_peer(i))
        for i in range(1, 8)
    ])
    rbuf[0] = rsrc[:, owned(z), :]
    rb = start([remote(lg.at[0], rb0, ss, sr, R0 + 10, partner)])
    arrive(s4)

    def attention(p, _):
        turned_k = kT[p]
        values = vp[p]
        query = qp[p]
        lines = []
        for e in range(2):
            h = 2 * p + e
            mine_q = masked(query, e)
            d = dout[h]
            mine_v = values[:, e * 128:(e + 1) * 128]
            low = (mix_of(h, 0, HALF, 0, ROWS) * nt(mine_v[:HALF], d)).astype(BF16)
            high = (mix_of(h, HALF, HALF, HALF, HALF) * nt(mine_v[HALF:], d[HALF:])).astype(BF16)
            key_low = nn(low, mine_q)
            key_high = nn(high, mine_q[HALF:])
            if e == 0:
                kacc[p, pl.ds(0, HALF), :] = key_low
                kacc[p, pl.ds(HALF, HALF), :] = key_high
            else:
                kacc[p, pl.ds(0, HALF), :] += key_low
                kacc[p, pl.ds(HALF, HALF), :] += key_high
            vacc[p, pl.ds(0, HALF), pl.ds(e * 128, 128)] = nn(sm[h, pl.ds(0, HALF), :], d)
            vacc[p, pl.ds(HALF, HALF), pl.ds(e * 128, 128)] = nn(
                sm[h, pl.ds(HALF, HALF), pl.ds(HALF, HALF)], d[HALF:]
            )
            own_k = turned_k[e * 64:(e + 1) * 64, :]
            line = nn(own_k[:, :HALF], low)
            line_high = nn(own_k[:, HALF:], high)
            at = pl.ds(pl.multiple_of(h * 64, 64), 64)
            states = state_low[:, at, :].reshape(SEQ_BITS * 64, 128)
            read = nt(states, d)
            for b in range(SEQ_BITS):
                line = line + lam[LB + 1 + b, pl.ds(h, 1), :] * read[b * 64:(b + 1) * 64, :]
            lines.append(jnp.concatenate([line[:, :HALF], line[:, HALF:] + line_high], axis=1))
        qo[p] = jnp.concatenate(lines, axis=0).T.astype(BF16)
        return 0

    lax.fori_loop(0, 2, attention, 0)
    arrive(r1x)
    tops = rbuf[0, pl.ds(3, 2)].astype(F32)
    for i in range(1, 8):
        tops = tops + rbuf[i, pl.ds(3, 2)].astype(F32)
    tsrc[...] = tops.astype(BF16)
    r2 = start([remote(tsrc, tbuf.at[i], ss, sr, R2 + i - 1, x_peer(i)) for i in range(1, 4)])

    lax.fori_loop(2, 4, attention, 0)
    arrive(r1)
    arrive(r2)
    outer = tbuf[1, 0].astype(F32) + tbuf[2, 1].astype(F32) + tbuf[3, 1].astype(F32)
    for r in range(8):
        total = outer
        for i in range(1, 8):
            total = total + rbuf[r ^ i, i.bit_length() - 1].astype(F32)
        rets[r] = total.astype(BF16)
    finals = pl.ds(pl.multiple_of(c * HALF + z * SLICE, SLICE), SLICE)
    r3 = start([remote(rets.at[i], rfin.at[finals], ss, sr, R3 + i - 1, z_peer(i)) for i in range(1, 8)])
    rfin[finals, :] = rets[0]
    arrive(rb)
    arrive(r3)
    r4 = start([remote(rfin.at[mine], rfin.at[mine], ss, sr, R4, partner)])
    arrive(r4)
    ret_ref[...] = (rfin[...].astype(F32) + rb0[...].astype(F32)).astype(BF16)
    for copy in sent:
        copy.wait_send()


def finish(back_ref, k_ref, v_ref, q_ref, kacc_ref, vacc_ref, qo_hbm, ko_hbm, vo_hbm, ko, vo, sem):
    copies = []

    def send(src, dst):
        copies.append(pltpu.make_async_copy(src, dst, sem.at[len(copies)]))
        copies[-1].start()

    for p in range(PAIRS):
        send(q_ref.at[p], qo_hbm.at[:, pl.ds(p * 128, 128)])
    zero = jnp.zeros((64, 128), BF16)
    for p in range(PAIRS):
        back = back_ref[pl.ds(p * 128, 128), :]
        spread = jnp.concatenate([
            jnp.concatenate([back[:64], zero], axis=1),
            jnp.concatenate([zero, back[64:]], axis=1),
        ], axis=0)
        vo[p] = (vacc_ref[p] + nn(k_ref[p], spread)).astype(BF16)
        send(vo.at[p], vo_hbm.at[:, pl.ds(p * 256, 256)])
        ko[p] = (kacc_ref[p] + nt(v_ref[p], spread)).astype(BF16)
        send(ko.at[p], ko_hbm.at[:, pl.ds(p * 128, 128)])
    for copy in copies:
        copy.wait()


def per_device(query_rows, key_rows, value_rows, out_grad, out_weight, level_codes, level_table):
    any_space = pl.BlockSpec(memory_space=pl.ANY)
    vmem = pl.BlockSpec(memory_space=pltpu.VMEM)
    scratch = [
        pltpu.VMEM((PAIRS, ROWS, 128), BF16),
        pltpu.VMEM((4, HEADS * DV, FEAT), BF16),
        pltpu.VMEM((4, ROWS, FEAT), BF16),
        pltpu.VMEM((HEADS, ROWS, DV), BF16),
        pltpu.VMEM((PAIRS, 128, ROWS), BF16),
        pltpu.VMEM((PAIRS, 128, ROWS), BF16),
        pltpu.VMEM((LB + 1 + SEQ_BITS, HEADS, ROWS), F32),
        pltpu.VMEM((ROWS // BLK, HEADS, ROWS), F32),
        pltpu.VMEM((HEADS, ROWS, ROWS), BF16),
        pltpu.VMEM((ROWS, 128), F32),
        pltpu.VMEM((ROWS, 128), F32),
        pltpu.VMEM((8, HALF, 128), BF16),
        pltpu.VMEM((4, HALF, 128), BF16),
        pltpu.VMEM((SEQ_BITS, ROWS, 128), BF16),
        pltpu.VMEM((SEQ_BITS, ROWS, 128), BF16),
        pltpu.VMEM((ROWS, 128), BF16),
        pltpu.VMEM((5, HALF, 128), BF16),
        pltpu.VMEM((5, HALF, 128), BF16),
        pltpu.VMEM((8, 5, SLICE, 128), BF16),
        pltpu.VMEM((2, SLICE, 128), BF16),
        pltpu.VMEM((4, 2, SLICE, 128), BF16),
        pltpu.VMEM((8, SLICE, 128), BF16),
        pltpu.VMEM((ROWS, 128), BF16),
        pltpu.VMEM((4, ROWS, 256), F32),
        pltpu.VMEM((PAIRS, 2, SEQ_BITS * 64, 128), F32),
        pltpu.VMEM((12, HEADS, ROWS), jnp.int32),
        pltpu.VMEM((HEADS, 16), F32),
        pltpu.SemaphoreType.DMA((19,)),
        pltpu.SemaphoreType.DMA((16,)),
        pltpu.SemaphoreType.DMA((16,)),
        pltpu.SemaphoreType.DMA((N_SEM,)),
        pltpu.SemaphoreType.DMA((N_SEM,)),
    ]
    inputs = [
        pltpu.with_memory_space_constraint(array, pltpu.HBM)
        for array in (query_rows, key_rows, value_rows, out_grad, out_weight, level_codes, level_table)
    ]
    queries, keys, values, returned, key_pairs, value_pairs = pl.pallas_call(
        kernel,
        out_shape=(
            pltpu.VMEM((PAIRS, ROWS, 128), BF16),
            pltpu.VMEM((PAIRS, ROWS, 128), F32),
            pltpu.VMEM((PAIRS, ROWS, 256), F32),
            pltpu.VMEM((ROWS, 128), BF16),
            pltpu.VMEM((PAIRS, ROWS, 128), BF16),
            pltpu.VMEM((PAIRS, ROWS, 256), BF16),
        ),
        in_specs=[any_space] * 7,
        out_specs=(vmem,) * 6,
        scratch_shapes=scratch,
        compiler_params=pltpu.CompilerParams(
            collective_id=0, has_side_effects=True, vmem_limit_bytes=40 * 1024 * 1024
        ),
        cost_estimate=pl.CostEstimate(flops=8_000_000_000, bytes_accessed=12_000_000, transcendentals=0),
    )(*inputs)
    return pl.pallas_call(
        finish,
        out_shape=(
            jax.ShapeDtypeStruct((ROWS, HEADS * DK), BF16),
            jax.ShapeDtypeStruct((ROWS, HEADS * DK), BF16),
            jax.ShapeDtypeStruct((ROWS, HEADS * DV), BF16),
        ),
        in_specs=[vmem] * 6,
        out_specs=(any_space,) * 3,
        scratch_shapes=[
            pltpu.VMEM((PAIRS, ROWS, 128), BF16),
            pltpu.VMEM((PAIRS, ROWS, 256), BF16),
            pltpu.SemaphoreType.DMA((3 * PAIRS,)),
        ],
        compiler_params=pltpu.CompilerParams(vmem_limit_bytes=16 * 1024 * 1024),
        cost_estimate=pl.CostEstimate(flops=500_000_000, bytes_accessed=8_000_000, transcendentals=0),
    )(returned, key_pairs, value_pairs, queries, keys, values)


def solution(mesh):
    return jax.shard_map(
        per_device,
        mesh=mesh,
        in_specs=(
            P("seq", "head"),
            P("seq", "head"),
            P("seq", "head"),
            P("seq", "head"),
            P("head", None),
            P(None, "head", "seq"),
            P("head", None),
        ),
        out_specs=(P("seq", "head"), P("seq", "head"), P("seq", "head")),
        check_vma=False,
    )
```

```python
import jax
import jax.numpy as jnp
from jax import lax
from jax.experimental import pallas as pl
from jax.experimental.pallas import tpu as pltpu
from jax.sharding import PartitionSpec as P

DK = 64
DV = 128
BLK = 64
LB = 3
SEQ_BITS = 6
ROWS = 512
HEADS = 8
PAIRS = 4
FEAT = 768
CHUNKS = 4
CROWS = ROWS // CHUNKS
HALF = 256
SLICE = 32
SCALES = [float((DK * BLK * 2 ** max(level - 1, 0)) ** -0.5) for level in range(LB + 1 + SEQ_BITS)]

F32 = jnp.float32
BF16 = jnp.bfloat16

S0, S1, S2, S4, R0, R1, R2, R3, N_SEM = 0, 1, 8, 11, 16, 27, 67, 70, 86
FAR_FIRST = (4, 5, 3, 7, 6, 2, 1)


def nt(a, b):
    return lax.dot_general(a, b, (((1,), (1,)), ((), ())), preferred_element_type=F32)


def nn(a, b):
    return lax.dot_general(a, b, (((1,), (0,)), ((), ())), preferred_element_type=F32)


def flipped(value, mask, bits):
    out = value
    for k in range(bits):
        if mask >> k & 1:
            out = out + (1 - 2 * ((value // 2**k) % 2)) * 2**k
    return out


def kernel(
    q_hbm, k_hbm, v_hbm, og_hbm, w_hbm, codes_hbm, table_hbm,
    qo, kacc, vacc, ret_ref, kp, vp,
    qp, w4, gath, dout, kT, qT, lam, inner, sm,
    gsb, pgs, zbuf, xbuf, state_low,
    lg, rb0, rbh, rsrc, rbuf, tsrc, tbuf, rets, rfin,
    pacc, lgacc, codes_ref, table_ref,
    loc_sem, ys, yr, ss, sr,
):
    g = lax.axis_index("seq")
    y = lax.axis_index("head")
    c = g % 2
    z = (g // 2) % 8
    x = g // 16
    right, left, across = (y + 1) % 4, (y + 3) % 4, (y + 2) % 4

    def z_peer(i):
        return (x * 16 + flipped(z, i, 3) * 2 + c, y)

    def z_other(i):
        return (x * 16 + flipped(z, i, 3) * 2 + 1 - c, y)

    def x_peer(i):
        return (flipped(x, i, 2) * 16 + z * 2 + c, y)

    partner = (g + 1 - 2 * c, y)
    def z_ring(step):
        return (x * 16 + ((z + step) % 8) * 2 + c, y)

    peers = [partner, (g, right), (g, left), z_ring(1), z_ring(7), x_peer(1), x_peer(3)]

    loads = []
    for p in range(PAIRS):
        loads.append(pltpu.make_async_copy(k_hbm.at[:, pl.ds(p * 128, 128)], kp.at[p], loc_sem.at[len(loads)]))
    for p in range(PAIRS):
        loads.append(pltpu.make_async_copy(v_hbm.at[:, pl.ds(p * 256, 256)], vp.at[p], loc_sem.at[len(loads)]))
    for p in range(PAIRS):
        loads.append(pltpu.make_async_copy(q_hbm.at[:, pl.ds(p * 128, 128)], qp.at[p], loc_sem.at[len(loads)]))
    loads.append(pltpu.make_async_copy(codes_hbm, codes_ref, loc_sem.at[len(loads)]))
    loads.append(pltpu.make_async_copy(table_hbm, table_ref, loc_sem.at[len(loads)]))
    loads.append(pltpu.make_async_copy(og_hbm, gath.at[y], loc_sem.at[len(loads)]))
    for p in range(4):
        loads.append(pltpu.make_async_copy(w_hbm.at[:, pl.ds(p * FEAT, FEAT)], w4.at[p], loc_sem.at[len(loads)]))
    for load in loads:
        load.start()

    rbuf[...] = jnp.zeros_like(rbuf)
    tbuf[...] = jnp.zeros_like(tbuf)

    barrier = pltpu.get_barrier_semaphore()
    for peer in peers:
        pl.semaphore_signal(barrier, inc=1, device_id=peer, device_id_type=pl.DeviceIdType.MESH)

    pl.semaphore_wait(barrier, len(peers))

    def remote(src, dst, send, recv, slot, to):
        return pltpu.make_async_remote_copy(
            src_ref=src, dst_ref=dst, send_sem=send.at[slot], recv_sem=recv.at[slot],
            device_id=to, device_id_type=pl.DeviceIdType.MESH,
        )

    def own(j):
        rows = pl.ds(j * CROWS, CROWS)
        return [
            remote(og_hbm.at[rows], gath.at[y, rows], ys, yr, j, (g, right)),
            remote(og_hbm.at[rows], gath.at[y, rows], ys, yr, 4 + j, (g, left)),
        ]

    def forward(j):
        first = pl.ds(j * CROWS, CROWS // 2)
        second = pl.ds(j * CROWS + CROWS // 2, CROWS // 2)
        return [
            remote(gath.at[left, first], gath.at[left, first], ys, yr, 8 + j, (g, right)),
            remote(gath.at[right, second], gath.at[right, second], ys, yr, 12 + j, (g, left)),
        ]

    def start(copies):
        for copy in copies:
            copy.start()
        sent.extend(copies)
        return copies

    def arrive(copies):
        for copy in copies:
            copy.wait_recv()

    def start_if(condition, copies):
        @pl.when(condition)
        def _():
            for copy in copies:
                copy.start()

        sent_if.append((condition, copies))

    def arrive_if(condition, copies):
        @pl.when(condition)
        def _():
            arrive(copies)

    sent, sent_if = [], []
    owns = [own(j) for j in range(CHUNKS)]
    forwards = [forward(j) for j in range(CHUNKS)]
    for j in range(CHUNKS):
        start(owns[j])
    for load in loads[:8]:
        load.wait()

    def states_of(p, _):
        kT[p] = kp[p].T
        both = nn(kT[p], vp[p])
        at = pl.multiple_of(p * 128, 128)
        gsb[pl.ds(at, 64), :] = both[:64, :128]
        gsb[pl.ds(at + 64, 64), :] = both[64:, 128:]
        return 0

    lax.fori_loop(0, PAIRS, states_of, 0)
    s0 = start([remote(gsb, pgs, ss, sr, S0, partner)])

    for load in loads[8:14]:
        load.wait()
    table = table_ref[...]
    columns = [jnp.broadcast_to(table[:, j:j + 1], (HEADS, ROWS)) for j in range(16)]
    for level in range(LB + 1 + SEQ_BITS):
        codes = codes_ref[level]
        looked = jnp.zeros((HEADS, ROWS), F32)
        for j in range(16):
            looked = jnp.where(codes == j, columns[j], looked)
        looked = looked * SCALES[level]
        if level > LB:
            looked = looked * ((g // 2 ** (level - LB - 1)) % 2).astype(F32)
        lam[level] = looked
    token_block = lax.broadcasted_iota(jnp.int32, (HEADS, ROWS), 1) // BLK
    for cs in range(ROWS // BLK):
        line = jnp.zeros((HEADS, ROWS), F32)
        for ct in range(cs, ROWS // BLK):
            line = jnp.where(token_block == ct, lam[(ct ^ cs).bit_length()], line)
        inner[cs] = line

    def turned(p, _):
        qT[p] = qp[p].T
        return 0

    lax.fori_loop(0, PAIRS, turned, 0)

    mine = pl.ds(pl.multiple_of(c * HALF, HALF), HALF)
    other = pl.ds(pl.multiple_of((1 - c) * HALF, HALF), HALF)
    arrive(s0)
    zbuf[z] = (gsb[mine, :] + pgs[mine, :]).astype(BF16)

    def ring(k):
        ahead, back = zbuf.at[(z + 8 - k) % 8], zbuf.at[(z + k) % 8]
        copies = [remote(ahead, ahead, ss, sr, S1 + k, z_ring(1))]
        if k < 3:
            copies.append(remote(back, back, ss, sr, S1 + 4 + k, z_ring(7)))
        return copies

    s1 = [ring(k) for k in range(4)]
    start(s1[0])
    state_low[0] = pgs[...].astype(BF16)

    def turn(j):
        arrive(owns[j])
        start(forwards[j])

    def mix_of(h, s0_, count, t0_, width):
        lines = [
            jnp.broadcast_to(inner[s0_ // BLK + i, pl.ds(h, 1), pl.ds(t0_, width)], (BLK, width))
            for i in range(count // BLK)
        ]
        mix = jnp.concatenate(lines, axis=0)
        s_at = lax.broadcasted_iota(jnp.int32, (count, width), 0) + s0_
        t_at = lax.broadcasted_iota(jnp.int32, (count, width), 1) + t0_
        return jnp.where(s_at <= t_at, mix, 0.0)

    def masked(pair, e):
        lane = lax.broadcasted_iota(jnp.int32, pair.shape, 1)
        return jnp.where((lane >= 64) == (e == 1), pair, jnp.zeros_like(pair))

    def scores_of(p, _):
        for e in range(2):
            h = 2 * p + e
            keys = masked(kp[p], e)
            query = qp[p]
            sm[h, pl.ds(0, HALF), :] = (mix_of(h, 0, HALF, 0, ROWS) * nt(keys[:HALF], query)).astype(BF16)
            sm[h, pl.ds(HALF, HALF), pl.ds(HALF, HALF)] = (
                mix_of(h, HALF, HALF, HALF, HALF) * nt(keys[HALF:], query[HALF:])
            ).astype(BF16)
        return 0

    lax.fori_loop(0, PAIRS, scores_of, 0)

    def project(slots, first, count, begin, end):
        def tile(n, _):
            cols = pl.ds(pl.multiple_of(n * 256, 256), 256)
            rows = pl.ds(first, count)
            total = None if begin else pacc[n, rows, :]
            for d in slots:
                part = nt(gath[d, rows, :], w4[d, cols, :])
                total = part if total is None else total + part
            if end:
                low = total.astype(BF16)
                dout[2 * n, rows, :] = low[:, :128]
                dout[2 * n + 1, rows, :] = low[:, 128:]
            else:
                pacc[n, rows, :] = total
            return 0

        lax.fori_loop(0, 4, tile, 0)

    def level_part(p, e, first, count):
        h = 2 * p + e
        rows = qT[p, e * 64:(e + 1) * 64, first:first + count].astype(F32)
        scaled = [
            (lam[LB + 1 + b, pl.ds(h, 1), :][:, first:first + count] * rows).astype(BF16) for b in range(SEQ_BITS)
        ]
        return nn(jnp.concatenate(scaled, axis=0), dout[h, first:first + count, :])

    def level_first(p, _):
        for e in range(2):
            lgacc[p, e] = level_part(p, e, 0, HALF)
        return 0

    def level_next(p, _):
        for e in range(2):
            lgacc[p, e] += level_part(p, e, HALF, CROWS)
        return 0

    def level_last(p):
        for e in range(2):
            grads = (lgacc[p, e] + level_part(p, e, HALF + CROWS, CROWS)).astype(BF16)
            at = pl.ds(pl.multiple_of(p * 128 + e * 64, 64), 64)
            for b in range(SEQ_BITS):
                lg[b, at, :] = grads[b * 64:(b + 1) * 64, :]

    for load in loads[14:]:
        load.wait()
    project([y], 0, ROWS, True, False)
    arrive(s1[0])
    start(s1[1])
    turn(0)
    arrive(s1[1])
    start(s1[2])
    turn(1)
    project([left, right], 0, HALF, False, False)
    arrive(s1[2])
    start(s1[3])
    turn(2)

    arrive(s1[3])
    parts = [zbuf[flipped(z, i, 3)].astype(F32) for i in range(8)]
    pair1 = parts[2] + parts[3]
    quad = (parts[4] + parts[5]) + (parts[6] + parts[7])
    xbuf[0] = ((parts[0] + parts[1]) + pair1 + quad).astype(BF16)
    s2 = start([remote(xbuf.at[0], xbuf.at[i], ss, sr, S2 + i - 1, x_peer(i)) for i in (1, 3)])
    state_low[1, mine, :] = parts[1].astype(BF16)
    state_low[2, mine, :] = pair1.astype(BF16)
    state_low[3, mine, :] = quad.astype(BF16)

    turn(3)
    arrive(s2)
    s2 = start([remote(xbuf.at[1], xbuf.at[2], ss, sr, S2 + 1, x_peer(3))])
    project([left, right], HALF, HALF, False, False)
    arrive(forwards[0])
    arrive(forwards[1])
    project([across], 0, HALF, False, True)
    lax.fori_loop(0, PAIRS, level_first, 0)

    arrive(s2)
    state_low[4, mine, :] = xbuf[1]
    state_low[5, mine, :] = (xbuf[2].astype(F32) + xbuf[3].astype(F32)).astype(BF16)
    s4 = start([
        remote(state_low.at[b, mine], state_low.at[b, mine], ss, sr, S4 + b - 1, partner) for b in range(1, SEQ_BITS)
    ])

    arrive(forwards[2])
    project([across], HALF, CROWS, False, True)
    lax.fori_loop(0, PAIRS, level_next, 0)
    arrive(forwards[3])
    project([across], HALF + CROWS, CROWS, False, True)

    r0 = []
    for i in range(2):
        p = 2 * (1 - c) + i
        level_last(p)
        rows = pl.ds(pl.multiple_of(p * 128, 128), 128)
        r0 += start([
            remote(lg.at[1 + b, rows], rbh.at[b, pl.ds(i * 128, 128)], ss, sr, R0 + 5 * i + b, partner)
            for b in range(5)
        ])
    for i in range(2):
        level_last(2 * c + i)
    arrive(r0)
    rsrc[...] = (lg[pl.ds(1, 5), mine, :].astype(F32) + rbh[...].astype(F32)).astype(BF16)

    def owned(at):
        return pl.ds(pl.multiple_of(at * SLICE, SLICE), SLICE)

    def slice_of(i, level):
        return remote(
            rsrc.at[level, owned(flipped(z, i, 3))], rbuf.at[i, level], ss, sr, R1 + 8 * level + i, z_peer(i)
        )

    upper = [x % 2 == 1, x // 2 == 1]
    for i in FAR_FIRST:
        for b in range(2):
            start_if(upper[b], [slice_of(i, 3 + b)])
    for i in FAR_FIRST:
        for b in range(3):
            start_if((z // 2**b) % 2 == 1, [slice_of(i, b)])
    rbuf[0] = rsrc[:, owned(z), :]
    rb = start([remote(lg.at[0], rb0, ss, sr, R0 + 10, partner)])
    arrive(s4)

    def attention(p, _):
        turned_k = kT[p]
        values = vp[p]
        query = qp[p]
        lines = []
        for e in range(2):
            h = 2 * p + e
            mine_q = masked(query, e)
            d = dout[h]
            mine_v = values[:, e * 128:(e + 1) * 128]
            low = (mix_of(h, 0, HALF, 0, ROWS) * nt(mine_v[:HALF], d)).astype(BF16)
            high = (mix_of(h, HALF, HALF, HALF, HALF) * nt(mine_v[HALF:], d[HALF:])).astype(BF16)
            key_low = nn(low, mine_q)
            key_high = nn(high, mine_q[HALF:])
            if e == 0:
                kacc[p, pl.ds(0, HALF), :] = key_low
                kacc[p, pl.ds(HALF, HALF), :] = key_high
            else:
                kacc[p, pl.ds(0, HALF), :] += key_low
                kacc[p, pl.ds(HALF, HALF), :] += key_high
            vacc[p, pl.ds(0, HALF), pl.ds(e * 128, 128)] = nn(sm[h, pl.ds(0, HALF), :], d)
            vacc[p, pl.ds(HALF, HALF), pl.ds(e * 128, 128)] = nn(
                sm[h, pl.ds(HALF, HALF), pl.ds(HALF, HALF)], d[HALF:]
            )
            own_k = turned_k[e * 64:(e + 1) * 64, :]
            line = nn(own_k[:, :HALF], low)
            line_high = nn(own_k[:, HALF:], high)
            at = pl.ds(pl.multiple_of(h * 64, 64), 64)
            states = state_low[:, at, :].reshape(SEQ_BITS * 64, 128)
            read = nt(states, d)
            for b in range(SEQ_BITS):
                line = line + lam[LB + 1 + b, pl.ds(h, 1), :] * read[b * 64:(b + 1) * 64, :]
            lines.append(jnp.concatenate([line[:, :HALF], line[:, HALF:] + line_high], axis=1))
        qo[p] = jnp.concatenate(lines, axis=0).T.astype(BF16)
        return 0

    lax.fori_loop(0, 2, attention, 0)
    for b in range(2):
        arrive_if(upper[b], [slice_of(i, 3 + b) for i in FAR_FIRST])
    tops = rbuf[0, pl.ds(3, 2)].astype(F32)
    for i in range(1, 8):
        tops = tops + rbuf[i, pl.ds(3, 2)].astype(F32)
    tsrc[...] = tops.astype(BF16)
    near = [remote(tsrc.at[0], tbuf.at[1, 0], ss, sr, R2, x_peer(1))]
    far = [remote(tsrc.at[1], tbuf.at[i, 1], ss, sr, R2 + i - 1, x_peer(i)) for i in (2, 3)]
    start_if(upper[1], far)
    start_if(upper[0], near)

    lax.fori_loop(2, 4, attention, 0)
    for i in FAR_FIRST:
        for b in range(3):
            arrive_if((flipped(z, i, 3) // 2**b) % 2 == 1, [slice_of(i, b)])
    arrive_if(x % 2 == 0, near)
    arrive_if(x // 2 == 0, far)
    outer = tbuf[1, 0].astype(F32) + tbuf[2, 1].astype(F32) + tbuf[3, 1].astype(F32)
    for r in range(8):
        total = outer
        for i in range(1, 8):
            total = total + rbuf[r ^ i, i.bit_length() - 1].astype(F32)
        rets[r] = total.astype(BF16)
    finals = pl.ds(pl.multiple_of(c * HALF + z * SLICE, SLICE), SLICE)
    r3 = []
    for i in FAR_FIRST:
        r3 += start([
            remote(rets.at[i], rfin.at[finals], ss, sr, R3 + i, z_peer(i)),
            remote(rets.at[i], rfin.at[finals], ss, sr, R3 + 8 + i, z_other(i)),
        ])
    r3 += start([remote(rets.at[0], rfin.at[finals], ss, sr, R3 + 8, partner)])
    rfin[finals, :] = rets[0]
    arrive(rb)
    arrive(r3)
    ret_ref[...] = (rfin[...].astype(F32) + rb0[...].astype(F32)).astype(BF16)
    for copy in sent:
        copy.wait_send()
    for condition, copies in sent_if:
        @pl.when(condition)
        def _(copies=copies):
            for copy in copies:
                copy.wait_send()


def finish(back_ref, k_ref, v_ref, q_ref, kacc_ref, vacc_ref, qo_hbm, ko_hbm, vo_hbm, ko, vo, sem):
    copies = []

    def send(src, dst):
        copies.append(pltpu.make_async_copy(src, dst, sem.at[len(copies)]))
        copies[-1].start()

    for p in range(PAIRS):
        send(q_ref.at[p], qo_hbm.at[:, pl.ds(p * 128, 128)])
    zero = jnp.zeros((64, 128), BF16)
    for p in range(PAIRS):
        back = back_ref[pl.ds(p * 128, 128), :]
        spread = jnp.concatenate([
            jnp.concatenate([back[:64], zero], axis=1),
            jnp.concatenate([zero, back[64:]], axis=1),
        ], axis=0)
        vo[p] = (vacc_ref[p] + nn(k_ref[p], spread)).astype(BF16)
        send(vo.at[p], vo_hbm.at[:, pl.ds(p * 256, 256)])
        ko[p] = (kacc_ref[p] + nt(v_ref[p], spread)).astype(BF16)
        send(ko.at[p], ko_hbm.at[:, pl.ds(p * 128, 128)])
    for copy in copies:
        copy.wait()


def per_device(query_rows, key_rows, value_rows, out_grad, out_weight, level_codes, level_table):
    any_space = pl.BlockSpec(memory_space=pl.ANY)
    vmem = pl.BlockSpec(memory_space=pltpu.VMEM)
    scratch = [
        pltpu.VMEM((PAIRS, ROWS, 128), BF16),
        pltpu.VMEM((4, HEADS * DV, FEAT), BF16),
        pltpu.VMEM((4, ROWS, FEAT), BF16),
        pltpu.VMEM((HEADS, ROWS, DV), BF16),
        pltpu.VMEM((PAIRS, 128, ROWS), BF16),
        pltpu.VMEM((PAIRS, 128, ROWS), BF16),
        pltpu.VMEM((LB + 1 + SEQ_BITS, HEADS, ROWS), F32),
        pltpu.VMEM((ROWS // BLK, HEADS, ROWS), F32),
        pltpu.VMEM((HEADS, ROWS, ROWS), BF16),
        pltpu.VMEM((ROWS, 128), F32),
        pltpu.VMEM((ROWS, 128), F32),
        pltpu.VMEM((8, HALF, 128), BF16),
        pltpu.VMEM((4, HALF, 128), BF16),
        pltpu.VMEM((SEQ_BITS, ROWS, 128), BF16),
        pltpu.VMEM((SEQ_BITS, ROWS, 128), BF16),
        pltpu.VMEM((ROWS, 128), BF16),
        pltpu.VMEM((5, HALF, 128), BF16),
        pltpu.VMEM((5, HALF, 128), BF16),
        pltpu.VMEM((8, 5, SLICE, 128), BF16),
        pltpu.VMEM((2, SLICE, 128), BF16),
        pltpu.VMEM((4, 2, SLICE, 128), BF16),
        pltpu.VMEM((8, SLICE, 128), BF16),
        pltpu.VMEM((ROWS, 128), BF16),
        pltpu.VMEM((4, ROWS, 256), F32),
        pltpu.VMEM((PAIRS, 2, SEQ_BITS * 64, 128), F32),
        pltpu.VMEM((12, HEADS, ROWS), jnp.int32),
        pltpu.VMEM((HEADS, 16), F32),
        pltpu.SemaphoreType.DMA((19,)),
        pltpu.SemaphoreType.DMA((16,)),
        pltpu.SemaphoreType.DMA((16,)),
        pltpu.SemaphoreType.DMA((N_SEM,)),
        pltpu.SemaphoreType.DMA((N_SEM,)),
    ]
    inputs = [
        pltpu.with_memory_space_constraint(array, pltpu.HBM)
        for array in (query_rows, key_rows, value_rows, out_grad, out_weight, level_codes, level_table)
    ]
    queries, keys, values, returned, key_pairs, value_pairs = pl.pallas_call(
        kernel,
        out_shape=(
            pltpu.VMEM((PAIRS, ROWS, 128), BF16),
            pltpu.VMEM((PAIRS, ROWS, 128), F32),
            pltpu.VMEM((PAIRS, ROWS, 256), F32),
            pltpu.VMEM((ROWS, 128), BF16),
            pltpu.VMEM((PAIRS, ROWS, 128), BF16),
            pltpu.VMEM((PAIRS, ROWS, 256), BF16),
        ),
        in_specs=[any_space] * 7,
        out_specs=(vmem,) * 6,
        scratch_shapes=scratch,
        compiler_params=pltpu.CompilerParams(
            collective_id=0, has_side_effects=True, vmem_limit_bytes=40 * 1024 * 1024
        ),
        cost_estimate=pl.CostEstimate(flops=8_000_000_000, bytes_accessed=12_000_000, transcendentals=0),
    )(*inputs)
    return pl.pallas_call(
        finish,
        out_shape=(
            jax.ShapeDtypeStruct((ROWS, HEADS * DK), BF16),
            jax.ShapeDtypeStruct((ROWS, HEADS * DK), BF16),
            jax.ShapeDtypeStruct((ROWS, HEADS * DV), BF16),
        ),
        in_specs=[vmem] * 6,
        out_specs=(any_space,) * 3,
        scratch_shapes=[
            pltpu.VMEM((PAIRS, ROWS, 128), BF16),
            pltpu.VMEM((PAIRS, ROWS, 256), BF16),
            pltpu.SemaphoreType.DMA((3 * PAIRS,)),
        ],
        compiler_params=pltpu.CompilerParams(vmem_limit_bytes=16 * 1024 * 1024),
        cost_estimate=pl.CostEstimate(flops=500_000_000, bytes_accessed=8_000_000, transcendentals=0),
    )(returned, key_pairs, value_pairs, queries, keys, values)


def solution(mesh):
    return jax.shard_map(
        per_device,
        mesh=mesh,
        in_specs=(
            P("seq", "head"),
            P("seq", "head"),
            P("seq", "head"),
            P("seq", "head"),
            P("head", None),
            P(None, "head", "seq"),
            P("head", None),
        ),
        out_specs=(P("seq", "head"), P("seq", "head"), P("seq", "head")),
        check_vma=False,
    )
```

```python
import jax
import jax.numpy as jnp
from jax import lax
from jax.experimental import pallas as pl
from jax.experimental.pallas import tpu as pltpu
from jax.sharding import PartitionSpec as P

DK = 64
DV = 128
BLK = 64
LB = 3
SEQ_BITS = 6
ROWS = 512
HEADS = 8
PAIRS = 4
FEAT = 768
CHUNKS = 4
CROWS = ROWS // CHUNKS
HALF = 256
SLICE = 32
SCALES = [float((DK * BLK * 2 ** max(level - 1, 0)) ** -0.5) for level in range(LB + 1 + SEQ_BITS)]

F32 = jnp.float32
BF16 = jnp.bfloat16

S0, S1, S2, S4, R0, R1, R2, R3, N_SEM = 0, 1, 8, 11, 16, 27, 67, 70, 86
FAR_FIRST = (4, 5, 3, 7, 6, 2, 1)


def nt(a, b):
    return lax.dot_general(a, b, (((1,), (1,)), ((), ())), preferred_element_type=F32)


def nn(a, b):
    return lax.dot_general(a, b, (((1,), (0,)), ((), ())), preferred_element_type=F32)


def flipped(value, mask, bits):
    out = value
    for k in range(bits):
        if mask >> k & 1:
            out = out + (1 - 2 * ((value // 2**k) % 2)) * 2**k
    return out


def kernel(
    q_hbm, k_hbm, v_hbm, og_hbm, w_hbm, codes_hbm, table_hbm,
    qo, kacc, vacc, ret_ref, kp, vp,
    qp, w4, gath, dout, kT, qT, lam, inner, sm,
    gsb, pgs, zbuf, xbuf, state_low,
    lg, rb0, rbh, rsrc, rbuf, tsrc, tbuf, rets, rfin,
    pacc, lgacc, codes_ref, table_ref,
    loc_sem, ys, yr, ss, sr,
):
    g = lax.axis_index("seq")
    y = lax.axis_index("head")
    c = g % 2
    z = (g // 2) % 8
    x = g // 16
    right, left, across = (y + 1) % 4, (y + 3) % 4, (y + 2) % 4

    def z_peer(i):
        return (x * 16 + flipped(z, i, 3) * 2 + c, y)

    def z_other(i):
        return (x * 16 + flipped(z, i, 3) * 2 + 1 - c, y)

    def x_peer(i):
        return (flipped(x, i, 2) * 16 + z * 2 + c, y)

    partner = (g + 1 - 2 * c, y)
    def z_ring(step):
        return (x * 16 + ((z + step) % 8) * 2 + c, y)

    peers = [partner, (g, right), (g, left), z_ring(1), z_ring(7), x_peer(1), x_peer(3)]

    barrier = pltpu.get_barrier_semaphore()
    for peer in peers:
        pl.semaphore_signal(barrier, inc=1, device_id=peer, device_id_type=pl.DeviceIdType.MESH)

    loads = []
    for p in range(PAIRS):
        loads.append(pltpu.make_async_copy(k_hbm.at[:, pl.ds(p * 128, 128)], kp.at[p], loc_sem.at[len(loads)]))
    for p in range(PAIRS):
        loads.append(pltpu.make_async_copy(v_hbm.at[:, pl.ds(p * 256, 256)], vp.at[p], loc_sem.at[len(loads)]))
    for p in range(PAIRS):
        loads.append(pltpu.make_async_copy(q_hbm.at[:, pl.ds(p * 128, 128)], qp.at[p], loc_sem.at[len(loads)]))
    loads.append(pltpu.make_async_copy(codes_hbm, codes_ref, loc_sem.at[len(loads)]))
    loads.append(pltpu.make_async_copy(table_hbm, table_ref, loc_sem.at[len(loads)]))
    loads.append(pltpu.make_async_copy(og_hbm, gath.at[y], loc_sem.at[len(loads)]))
    for p in range(4):
        loads.append(pltpu.make_async_copy(w_hbm.at[:, pl.ds(p * FEAT, FEAT)], w4.at[p], loc_sem.at[len(loads)]))
    pl.semaphore_wait(barrier, len(peers))

    def remote(src, dst, send, recv, slot, to):
        return pltpu.make_async_remote_copy(
            src_ref=src, dst_ref=dst, send_sem=send.at[slot], recv_sem=recv.at[slot],
            device_id=to, device_id_type=pl.DeviceIdType.MESH,
        )

    def own(j):
        rows = pl.ds(j * CROWS, CROWS)
        return [
            remote(og_hbm.at[rows], gath.at[y, rows], ys, yr, j, (g, right)),
            remote(og_hbm.at[rows], gath.at[y, rows], ys, yr, 4 + j, (g, left)),
        ]

    def forward(j):
        first = pl.ds(j * CROWS, CROWS // 2)
        second = pl.ds(j * CROWS + CROWS // 2, CROWS // 2)
        return [
            remote(gath.at[left, first], gath.at[left, first], ys, yr, 8 + j, (g, right)),
            remote(gath.at[right, second], gath.at[right, second], ys, yr, 12 + j, (g, left)),
        ]

    def start(copies):
        for copy in copies:
            copy.start()
        sent.extend(copies)
        return copies

    def arrive(copies):
        for copy in copies:
            copy.wait_recv()

    def start_if(condition, copies):
        @pl.when(condition)
        def _():
            for copy in copies:
                copy.start()

        sent_if.append((condition, copies))

    def arrive_if(condition, copies):
        @pl.when(condition)
        def _():
            arrive(copies)

    sent, sent_if = [], []
    owns = [own(j) for j in range(CHUNKS)]
    forwards = [forward(j) for j in range(CHUNKS)]
    for j in range(CHUNKS):
        start(owns[j])
    for load in loads:
        load.start()
    rbuf[...] = jnp.zeros_like(rbuf)
    tbuf[...] = jnp.zeros_like(tbuf)
    for load in loads[:8]:
        load.wait()

    def states_of(p, _):
        kT[p] = kp[p].T
        both = nn(kT[p], vp[p])
        at = pl.multiple_of(p * 128, 128)
        gsb[pl.ds(at, 64), :] = both[:64, :128]
        gsb[pl.ds(at + 64, 64), :] = both[64:, 128:]
        return 0

    lax.fori_loop(0, PAIRS, states_of, 0)
    s0 = start([remote(gsb, pgs, ss, sr, S0, partner)])

    for load in loads[8:14]:
        load.wait()
    table = table_ref[...]
    columns = [jnp.broadcast_to(table[:, j:j + 1], (HEADS, ROWS)) for j in range(16)]
    for level in range(LB + 1 + SEQ_BITS):
        codes = codes_ref[level]
        looked = jnp.zeros((HEADS, ROWS), F32)
        for j in range(16):
            looked = jnp.where(codes == j, columns[j], looked)
        looked = looked * SCALES[level]
        if level > LB:
            looked = looked * ((g // 2 ** (level - LB - 1)) % 2).astype(F32)
        lam[level] = looked
    token_block = lax.broadcasted_iota(jnp.int32, (HEADS, ROWS), 1) // BLK
    for cs in range(ROWS // BLK):
        line = jnp.zeros((HEADS, ROWS), F32)
        for ct in range(cs, ROWS // BLK):
            line = jnp.where(token_block == ct, lam[(ct ^ cs).bit_length()], line)
        inner[cs] = line

    def turned(p, _):
        qT[p] = qp[p].T
        return 0

    lax.fori_loop(0, PAIRS, turned, 0)

    mine = pl.ds(pl.multiple_of(c * HALF, HALF), HALF)
    other = pl.ds(pl.multiple_of((1 - c) * HALF, HALF), HALF)
    arrive(s0)
    zbuf[z] = (gsb[mine, :] + pgs[mine, :]).astype(BF16)

    def ring(k):
        ahead, back = zbuf.at[(z + 8 - k) % 8], zbuf.at[(z + k) % 8]
        copies = [remote(ahead, ahead, ss, sr, S1 + k, z_ring(1))]
        if k < 3:
            copies.append(remote(back, back, ss, sr, S1 + 4 + k, z_ring(7)))
        return copies

    s1 = [ring(k) for k in range(4)]
    start(s1[0])
    state_low[0] = pgs[...].astype(BF16)

    def turn(j):
        arrive(owns[j])
        start(forwards[j])

    def mix_of(h, s0_, count, t0_, width):
        lines = [
            jnp.broadcast_to(inner[s0_ // BLK + i, pl.ds(h, 1), pl.ds(t0_, width)], (BLK, width))
            for i in range(count // BLK)
        ]
        mix = jnp.concatenate(lines, axis=0)
        s_at = lax.broadcasted_iota(jnp.int32, (count, width), 0) + s0_
        t_at = lax.broadcasted_iota(jnp.int32, (count, width), 1) + t0_
        return jnp.where(s_at <= t_at, mix, 0.0)

    def masked(pair, e):
        lane = lax.broadcasted_iota(jnp.int32, pair.shape, 1)
        return jnp.where((lane >= 64) == (e == 1), pair, jnp.zeros_like(pair))

    def scores_of(p, _):
        for e in range(2):
            h = 2 * p + e
            keys = masked(kp[p], e)
            query = qp[p]
            sm[h, pl.ds(0, HALF), :] = (mix_of(h, 0, HALF, 0, ROWS) * nt(keys[:HALF], query)).astype(BF16)
            sm[h, pl.ds(HALF, HALF), pl.ds(HALF, HALF)] = (
                mix_of(h, HALF, HALF, HALF, HALF) * nt(keys[HALF:], query[HALF:])
            ).astype(BF16)
        return 0

    lax.fori_loop(0, PAIRS, scores_of, 0)

    def project_pair(n, slots, first, count, begin, end):
        cols = pl.ds(pl.multiple_of(n * 256, 256), 256)
        rows = pl.ds(first, count)
        total = None if begin else pacc[n, rows, :]
        for d in slots:
            part = nt(gath[d, rows, :], w4[d, cols, :])
            total = part if total is None else total + part
        if end:
            low = total.astype(BF16)
            dout[2 * n, rows, :] = low[:, :128]
            dout[2 * n + 1, rows, :] = low[:, 128:]
        else:
            pacc[n, rows, :] = total

    def project(*how):
        for n in range(PAIRS):
            project_pair(n, *how)

    def level_part(p, e, first, count):
        h = 2 * p + e
        rows = qT[p, e * 64:(e + 1) * 64, first:first + count].astype(F32)
        scaled = [
            (lam[LB + 1 + b, pl.ds(h, 1), :][:, first:first + count] * rows).astype(BF16) for b in range(SEQ_BITS)
        ]
        return nn(jnp.concatenate(scaled, axis=0), dout[h, first:first + count, :])

    def level_first(p, _):
        for e in range(2):
            lgacc[p, e] = level_part(p, e, 0, HALF)
        return 0

    def level_last(p):
        for e in range(2):
            grads = (lgacc[p, e] + level_part(p, e, HALF, HALF)).astype(BF16)
            at = pl.ds(pl.multiple_of(p * 128 + e * 64, 64), 64)
            for b in range(SEQ_BITS):
                lg[b, at, :] = grads[b * 64:(b + 1) * 64, :]

    for load in loads[14:]:
        load.wait()
    project([y], 0, ROWS, True, False)
    arrive(s1[0])
    start(s1[1])
    turn(0)
    arrive(s1[1])
    start(s1[2])
    turn(1)
    project([left, right], 0, HALF, False, False)
    arrive(s1[2])
    start(s1[3])
    turn(2)

    arrive(s1[3])
    parts = [zbuf[flipped(z, i, 3)].astype(F32) for i in range(8)]
    pair1 = parts[2] + parts[3]
    quad = (parts[4] + parts[5]) + (parts[6] + parts[7])
    xbuf[0] = ((parts[0] + parts[1]) + pair1 + quad).astype(BF16)
    s2 = start([remote(xbuf.at[0], xbuf.at[i], ss, sr, S2 + i - 1, x_peer(i)) for i in (1, 3)])
    state_low[1, mine, :] = parts[1].astype(BF16)
    state_low[2, mine, :] = pair1.astype(BF16)
    state_low[3, mine, :] = quad.astype(BF16)

    turn(3)
    arrive(s2)
    s2 = start([remote(xbuf.at[1], xbuf.at[2], ss, sr, S2 + 1, x_peer(3))])
    project([left, right], HALF, HALF, False, False)
    arrive(forwards[0])
    arrive(forwards[1])
    project([across], 0, HALF, False, True)
    lax.fori_loop(0, PAIRS, level_first, 0, unroll=True)

    arrive(forwards[2])
    project([across], HALF, CROWS, False, True)
    arrive(forwards[3])
    project([across], HALF + CROWS, CROWS, False, True)

    r0 = []
    for i in range(2):
        p = 2 * (1 - c) + i
        level_last(p)
        rows = pl.ds(pl.multiple_of(p * 128, 128), 128)
        r0 += start([
            remote(lg.at[1 + b, rows], rbh.at[b, pl.ds(i * 128, 128)], ss, sr, R0 + 5 * i + b, partner)
            for b in range(5)
        ])
    for i in range(2):
        level_last(2 * c + i)
    arrive(r0)
    rsrc[...] = (lg[pl.ds(1, 5), mine, :].astype(F32) + rbh[...].astype(F32)).astype(BF16)

    def owned(at):
        return pl.ds(pl.multiple_of(at * SLICE, SLICE), SLICE)

    def slice_of(i, level):
        return remote(
            rsrc.at[level, owned(flipped(z, i, 3))], rbuf.at[i, level], ss, sr, R1 + 8 * level + i, z_peer(i)
        )

    upper = [x % 2 == 1, x // 2 == 1]
    for i in FAR_FIRST:
        for b in range(2):
            start_if(upper[b], [slice_of(i, 3 + b)])
    for i in FAR_FIRST:
        for b in range(3):
            start_if((z // 2**b) % 2 == 1, [slice_of(i, b)])
    rbuf[0] = rsrc[:, owned(z), :]
    rb = start([remote(lg.at[0], rb0, ss, sr, R0 + 10, partner)])
    arrive(s2)
    state_low[4, mine, :] = xbuf[1]
    state_low[5, mine, :] = (xbuf[2].astype(F32) + xbuf[3].astype(F32)).astype(BF16)
    s4 = start([
        remote(state_low.at[b, mine], state_low.at[b, mine], ss, sr, S4 + b - 1, partner) for b in range(1, SEQ_BITS)
    ])
    arrive(s4)

    def attention(p, _):
        turned_k = kT[p]
        values = vp[p]
        query = qp[p]
        lines = []
        for e in range(2):
            h = 2 * p + e
            mine_q = masked(query, e)
            d = dout[h]
            mine_v = values[:, e * 128:(e + 1) * 128]
            low = (mix_of(h, 0, HALF, 0, ROWS) * nt(mine_v[:HALF], d)).astype(BF16)
            high = (mix_of(h, HALF, HALF, HALF, HALF) * nt(mine_v[HALF:], d[HALF:])).astype(BF16)
            key_low = nn(low, mine_q)
            key_high = nn(high, mine_q[HALF:])
            if e == 0:
                kacc[p, pl.ds(0, HALF), :] = key_low
                kacc[p, pl.ds(HALF, HALF), :] = key_high
            else:
                kacc[p, pl.ds(0, HALF), :] += key_low
                kacc[p, pl.ds(HALF, HALF), :] += key_high
            vacc[p, pl.ds(0, HALF), pl.ds(e * 128, 128)] = nn(sm[h, pl.ds(0, HALF), :], d)
            vacc[p, pl.ds(HALF, HALF), pl.ds(e * 128, 128)] = nn(
                sm[h, pl.ds(HALF, HALF), pl.ds(HALF, HALF)], d[HALF:]
            )
            own_k = turned_k[e * 64:(e + 1) * 64, :]
            line = nn(own_k[:, :HALF], low)
            line_high = nn(own_k[:, HALF:], high)
            at = pl.ds(pl.multiple_of(h * 64, 64), 64)
            states = state_low[:, at, :].reshape(SEQ_BITS * 64, 128)
            read = nt(states, d)
            for b in range(SEQ_BITS):
                line = line + lam[LB + 1 + b, pl.ds(h, 1), :] * read[b * 64:(b + 1) * 64, :]
            lines.append(jnp.concatenate([line[:, :HALF], line[:, HALF:] + line_high], axis=1))
        qo[p] = jnp.concatenate(lines, axis=0).T.astype(BF16)
        return 0

    lax.fori_loop(0, 2, attention, 0)
    for b in range(2):
        arrive_if(upper[b], [slice_of(i, 3 + b) for i in FAR_FIRST])
    tops = rbuf[0, pl.ds(3, 2)].astype(F32)
    for i in range(1, 8):
        tops = tops + rbuf[i, pl.ds(3, 2)].astype(F32)
    tsrc[...] = tops.astype(BF16)
    near = [remote(tsrc.at[0], tbuf.at[1, 0], ss, sr, R2, x_peer(1))]
    far = [remote(tsrc.at[1], tbuf.at[i, 1], ss, sr, R2 + i - 1, x_peer(i)) for i in (2, 3)]
    start_if(upper[1], far)
    start_if(upper[0], near)

    lax.fori_loop(2, 4, attention, 0)
    for i in FAR_FIRST:
        for b in range(3):
            arrive_if((flipped(z, i, 3) // 2**b) % 2 == 1, [slice_of(i, b)])
    arrive_if(x % 2 == 0, near)
    arrive_if(x // 2 == 0, far)
    outer = tbuf[1, 0].astype(F32) + tbuf[2, 1].astype(F32) + tbuf[3, 1].astype(F32)
    finals = pl.ds(pl.multiple_of(c * HALF + z * SLICE, SLICE), SLICE)
    r3 = []
    for r in FAR_FIRST + (0,):
        total = outer
        for i in range(1, 8):
            total = total + rbuf[r ^ i, i.bit_length() - 1].astype(F32)
        rets[r] = total.astype(BF16)
        if r:
            r3 += start([remote(rets.at[r], rfin.at[finals], ss, sr, R3 + r, z_peer(r))])
        r3 += start([remote(rets.at[r], rfin.at[finals], ss, sr, R3 + 8 + r, z_other(r) if r else partner)])
    rfin[finals, :] = rets[0]
    arrive(rb)
    arrive(r3)
    ret_ref[...] = (rfin[...].astype(F32) + rb0[...].astype(F32)).astype(BF16)
    for copy in sent:
        copy.wait_send()
    for condition, copies in sent_if:
        @pl.when(condition)
        def _(copies=copies):
            for copy in copies:
                copy.wait_send()


def finish(back_ref, k_ref, v_ref, q_ref, kacc_ref, vacc_ref, qo_hbm, ko_hbm, vo_hbm, ko, vo, sem):
    copies = []

    def send(src, dst):
        copies.append(pltpu.make_async_copy(src, dst, sem.at[len(copies)]))
        copies[-1].start()

    for p in range(PAIRS):
        send(q_ref.at[p], qo_hbm.at[:, pl.ds(p * 128, 128)])
    zero = jnp.zeros((64, 128), BF16)
    for p in range(PAIRS):
        back = back_ref[pl.ds(p * 128, 128), :]
        spread = jnp.concatenate([
            jnp.concatenate([back[:64], zero], axis=1),
            jnp.concatenate([zero, back[64:]], axis=1),
        ], axis=0)
        vo[p] = (vacc_ref[p] + nn(k_ref[p], spread)).astype(BF16)
        send(vo.at[p], vo_hbm.at[:, pl.ds(p * 256, 256)])
        ko[p] = (kacc_ref[p] + nt(v_ref[p], spread)).astype(BF16)
        send(ko.at[p], ko_hbm.at[:, pl.ds(p * 128, 128)])
    for copy in copies:
        copy.wait()


def per_device(query_rows, key_rows, value_rows, out_grad, out_weight, level_codes, level_table):
    any_space = pl.BlockSpec(memory_space=pl.ANY)
    vmem = pl.BlockSpec(memory_space=pltpu.VMEM)
    scratch = [
        pltpu.VMEM((PAIRS, ROWS, 128), BF16),
        pltpu.VMEM((4, HEADS * DV, FEAT), BF16),
        pltpu.VMEM((4, ROWS, FEAT), BF16),
        pltpu.VMEM((HEADS, ROWS, DV), BF16),
        pltpu.VMEM((PAIRS, 128, ROWS), BF16),
        pltpu.VMEM((PAIRS, 128, ROWS), BF16),
        pltpu.VMEM((LB + 1 + SEQ_BITS, HEADS, ROWS), F32),
        pltpu.VMEM((ROWS // BLK, HEADS, ROWS), F32),
        pltpu.VMEM((HEADS, ROWS, ROWS), BF16),
        pltpu.VMEM((ROWS, 128), F32),
        pltpu.VMEM((ROWS, 128), F32),
        pltpu.VMEM((8, HALF, 128), BF16),
        pltpu.VMEM((4, HALF, 128), BF16),
        pltpu.VMEM((SEQ_BITS, ROWS, 128), BF16),
        pltpu.VMEM((SEQ_BITS, ROWS, 128), BF16),
        pltpu.VMEM((ROWS, 128), BF16),
        pltpu.VMEM((5, HALF, 128), BF16),
        pltpu.VMEM((5, HALF, 128), BF16),
        pltpu.VMEM((8, 5, SLICE, 128), BF16),
        pltpu.VMEM((2, SLICE, 128), BF16),
        pltpu.VMEM((4, 2, SLICE, 128), BF16),
        pltpu.VMEM((8, SLICE, 128), BF16),
        pltpu.VMEM((ROWS, 128), BF16),
        pltpu.VMEM((4, ROWS, 256), F32),
        pltpu.VMEM((PAIRS, 2, SEQ_BITS * 64, 128), F32),
        pltpu.VMEM((12, HEADS, ROWS), jnp.int32),
        pltpu.VMEM((HEADS, 16), F32),
        pltpu.SemaphoreType.DMA((19,)),
        pltpu.SemaphoreType.DMA((16,)),
        pltpu.SemaphoreType.DMA((16,)),
        pltpu.SemaphoreType.DMA((N_SEM,)),
        pltpu.SemaphoreType.DMA((N_SEM,)),
    ]
    inputs = [
        pltpu.with_memory_space_constraint(array, pltpu.HBM)
        for array in (query_rows, key_rows, value_rows, out_grad, out_weight, level_codes, level_table)
    ]
    queries, keys, values, returned, key_pairs, value_pairs = pl.pallas_call(
        kernel,
        out_shape=(
            pltpu.VMEM((PAIRS, ROWS, 128), BF16),
            pltpu.VMEM((PAIRS, ROWS, 128), F32),
            pltpu.VMEM((PAIRS, ROWS, 256), F32),
            pltpu.VMEM((ROWS, 128), BF16),
            pltpu.VMEM((PAIRS, ROWS, 128), BF16),
            pltpu.VMEM((PAIRS, ROWS, 256), BF16),
        ),
        in_specs=[any_space] * 7,
        out_specs=(vmem,) * 6,
        scratch_shapes=scratch,
        compiler_params=pltpu.CompilerParams(
            collective_id=0, has_side_effects=True, vmem_limit_bytes=40 * 1024 * 1024
        ),
        cost_estimate=pl.CostEstimate(flops=8_000_000_000, bytes_accessed=12_000_000, transcendentals=0),
    )(*inputs)
    return pl.pallas_call(
        finish,
        out_shape=(
            jax.ShapeDtypeStruct((ROWS, HEADS * DK), BF16),
            jax.ShapeDtypeStruct((ROWS, HEADS * DK), BF16),
            jax.ShapeDtypeStruct((ROWS, HEADS * DV), BF16),
        ),
        in_specs=[vmem] * 6,
        out_specs=(any_space,) * 3,
        scratch_shapes=[
            pltpu.VMEM((PAIRS, ROWS, 128), BF16),
            pltpu.VMEM((PAIRS, ROWS, 256), BF16),
            pltpu.SemaphoreType.DMA((3 * PAIRS,)),
        ],
        compiler_params=pltpu.CompilerParams(vmem_limit_bytes=16 * 1024 * 1024),
        cost_estimate=pl.CostEstimate(flops=500_000_000, bytes_accessed=8_000_000, transcendentals=0),
    )(returned, key_pairs, value_pairs, queries, keys, values)


def solution(mesh):
    return jax.shard_map(
        per_device,
        mesh=mesh,
        in_specs=(
            P("seq", "head"),
            P("seq", "head"),
            P("seq", "head"),
            P("seq", "head"),
            P("head", None),
            P(None, "head", "seq"),
            P("head", None),
        ),
        out_specs=(P("seq", "head"), P("seq", "head"), P("seq", "head")),
        check_vma=False,
    )
```

```python
import jax
import jax.numpy as jnp
from jax import lax
from jax.experimental import pallas as pl
from jax.experimental.pallas import tpu as pltpu
from jax.sharding import PartitionSpec as P

DK = 64
DV = 128
BLK = 64
LB = 3
SEQ_BITS = 6
ROWS = 512
HEADS = 8
PAIRS = 4
FEAT = 768
CHUNKS = 4
CROWS = ROWS // CHUNKS
HALF = 256
SLICE = 32
SCALES = [float((DK * BLK * 2 ** max(level - 1, 0)) ** -0.5) for level in range(LB + 1 + SEQ_BITS)]

F32 = jnp.float32
BF16 = jnp.bfloat16

S0, S1, S2, S4, R0, R1, R2, R3, N_SEM = 0, 1, 8, 11, 16, 27, 32, 35, 36
FAR_FIRST = (4, 5, 3, 7, 6, 2, 1)


def nt(a, b):
    return lax.dot_general(a, b, (((1,), (1,)), ((), ())), preferred_element_type=F32)


def nn(a, b):
    return lax.dot_general(a, b, (((1,), (0,)), ((), ())), preferred_element_type=F32)


def flipped(value, mask, bits):
    out = value
    for k in range(bits):
        if mask >> k & 1:
            out = out + (1 - 2 * ((value // 2**k) % 2)) * 2**k
    return out


def kernel(
    q_hbm, k_hbm, v_hbm, og_hbm, w_hbm, codes_hbm, table_hbm,
    qo, kacc, vacc, ret_ref, kp, vp,
    qp, w4, gath, dout, kT, qT, lam, inner, sm,
    gsb, pgs, zbuf, xbuf, state_low,
    lg, rb0, rbh, rsrc, rbuf, tsrc, tbuf, rets, rfin,
    pacc, lgacc, rest, codes_ref, table_ref,
    loc_sem, ys, yr, ss, sr,
):
    g = lax.axis_index("seq")
    y = lax.axis_index("head")
    c = g % 2
    z = (g // 2) % 8
    x = g // 16
    right, left, across = (y + 1) % 4, (y + 3) % 4, (y + 2) % 4

    def z_peer(i):
        return (x * 16 + flipped(z, i, 3) * 2 + c, y)

    def z_other(i):
        return (x * 16 + flipped(z, i, 3) * 2 + 1 - c, y)

    def x_peer(i):
        return (flipped(x, i, 2) * 16 + z * 2 + c, y)

    partner = (g + 1 - 2 * c, y)
    def z_ring(step):
        return (x * 16 + ((z + step) % 8) * 2 + c, y)

    peers = [partner, (g, right), (g, left), z_ring(1), z_ring(7), x_peer(1), x_peer(3)]

    barrier = pltpu.get_barrier_semaphore()
    for peer in peers:
        pl.semaphore_signal(barrier, inc=1, device_id=peer, device_id_type=pl.DeviceIdType.MESH)

    loads = []
    for p in range(PAIRS):
        loads.append(pltpu.make_async_copy(k_hbm.at[:, pl.ds(p * 128, 128)], kp.at[p], loc_sem.at[len(loads)]))
    for p in range(PAIRS):
        loads.append(pltpu.make_async_copy(v_hbm.at[:, pl.ds(p * 256, 256)], vp.at[p], loc_sem.at[len(loads)]))
    for p in range(PAIRS):
        loads.append(pltpu.make_async_copy(q_hbm.at[:, pl.ds(p * 128, 128)], qp.at[p], loc_sem.at[len(loads)]))
    loads.append(pltpu.make_async_copy(codes_hbm, codes_ref, loc_sem.at[len(loads)]))
    loads.append(pltpu.make_async_copy(table_hbm, table_ref, loc_sem.at[len(loads)]))
    loads.append(pltpu.make_async_copy(og_hbm, gath.at[y], loc_sem.at[len(loads)]))
    for p in range(4):
        loads.append(pltpu.make_async_copy(w_hbm.at[:, pl.ds(p * FEAT, FEAT)], w4.at[p], loc_sem.at[len(loads)]))
    pl.semaphore_wait(barrier, len(peers))

    def remote(src, dst, send, recv, slot, to):
        return pltpu.make_async_remote_copy(
            src_ref=src, dst_ref=dst, send_sem=send.at[slot], recv_sem=recv.at[slot],
            device_id=to, device_id_type=pl.DeviceIdType.MESH,
        )

    def own(j):
        rows = pl.ds(j * CROWS, CROWS)
        return [
            remote(og_hbm.at[rows], gath.at[y, rows], ys, yr, j, (g, right)),
            remote(og_hbm.at[rows], gath.at[y, rows], ys, yr, 4 + j, (g, left)),
        ]

    def forward(j):
        first = pl.ds(j * CROWS, CROWS // 2)
        second = pl.ds(j * CROWS + CROWS // 2, CROWS // 2)
        return [
            remote(gath.at[left, first], gath.at[left, first], ys, yr, 8 + j, (g, right)),
            remote(gath.at[right, second], gath.at[right, second], ys, yr, 12 + j, (g, left)),
        ]

    def start(copies):
        for copy in copies:
            copy.start()
        sent.extend(copies)
        return copies

    def arrive(copies):
        for copy in copies:
            copy.wait_recv()

    def start_if(condition, copies):
        @pl.when(condition)
        def _():
            for copy in copies:
                copy.start()

        sent_if.append((condition, copies))

    def arrive_if(condition, copies):
        @pl.when(condition)
        def _():
            arrive(copies)

    sent, sent_if = [], []
    owns = [own(j) for j in range(CHUNKS)]
    forwards = [forward(j) for j in range(CHUNKS)]
    for j in range(CHUNKS):
        start(owns[j])
    for load in loads:
        load.start()
    rbuf[...] = jnp.zeros_like(rbuf)
    tbuf[...] = jnp.zeros_like(tbuf)
    for load in loads[:8]:
        load.wait()

    def states_of(p, _):
        kT[p] = kp[p].T
        both = nn(kT[p], vp[p])
        at = pl.multiple_of(p * 128, 128)
        gsb[pl.ds(at, 64), :] = both[:64, :128]
        gsb[pl.ds(at + 64, 64), :] = both[64:, 128:]
        return 0

    lax.fori_loop(0, PAIRS, states_of, 0)
    s0 = start([remote(gsb, pgs, ss, sr, S0, partner)])

    for load in loads[8:14]:
        load.wait()
    table = table_ref[...]
    columns = [jnp.broadcast_to(table[:, j:j + 1], (HEADS, ROWS)) for j in range(16)]
    for level in range(LB + 1 + SEQ_BITS):
        codes = codes_ref[level]
        looked = jnp.zeros((HEADS, ROWS), F32)
        for j in range(16):
            looked = jnp.where(codes == j, columns[j], looked)
        looked = looked * SCALES[level]
        if level > LB:
            looked = looked * ((g // 2 ** (level - LB - 1)) % 2).astype(F32)
        lam[level] = looked
    token_block = lax.broadcasted_iota(jnp.int32, (HEADS, ROWS), 1) // BLK
    for cs in range(ROWS // BLK):
        line = jnp.zeros((HEADS, ROWS), F32)
        for ct in range(cs, ROWS // BLK):
            line = jnp.where(token_block == ct, lam[(ct ^ cs).bit_length()], line)
        inner[cs] = line

    def turned(p, _):
        qT[p] = qp[p].T
        return 0

    lax.fori_loop(0, PAIRS, turned, 0)

    mine = pl.ds(pl.multiple_of(c * HALF, HALF), HALF)
    other = pl.ds(pl.multiple_of((1 - c) * HALF, HALF), HALF)
    arrive(s0)
    zbuf[z] = (gsb[mine, :] + pgs[mine, :]).astype(BF16)

    def ring(k):
        ahead, back = zbuf.at[(z + 8 - k) % 8], zbuf.at[(z + k) % 8]
        copies = [remote(ahead, ahead, ss, sr, S1 + k, z_ring(1))]
        if k < 3:
            copies.append(remote(back, back, ss, sr, S1 + 4 + k, z_ring(7)))
        return copies

    s1 = [ring(k) for k in range(4)]
    start(s1[0])
    state_low[0] = pgs[...].astype(BF16)

    def turn(j):
        arrive(owns[j])
        start(forwards[j])

    def mix_of(h, s0_, count, t0_, width):
        lines = [
            jnp.broadcast_to(inner[s0_ // BLK + i, pl.ds(h, 1), pl.ds(t0_, width)], (BLK, width))
            for i in range(count // BLK)
        ]
        mix = jnp.concatenate(lines, axis=0)
        s_at = lax.broadcasted_iota(jnp.int32, (count, width), 0) + s0_
        t_at = lax.broadcasted_iota(jnp.int32, (count, width), 1) + t0_
        return jnp.where(s_at <= t_at, mix, 0.0)

    def masked(pair, e):
        lane = lax.broadcasted_iota(jnp.int32, pair.shape, 1)
        return jnp.where((lane >= 64) == (e == 1), pair, jnp.zeros_like(pair))

    def scores_of(p, _):
        for e in range(2):
            h = 2 * p + e
            keys = masked(kp[p], e)
            query = qp[p]
            sm[h, pl.ds(0, HALF), :] = (mix_of(h, 0, HALF, 0, ROWS) * nt(keys[:HALF], query)).astype(BF16)
            sm[h, pl.ds(HALF, HALF), pl.ds(HALF, HALF)] = (
                mix_of(h, HALF, HALF, HALF, HALF) * nt(keys[HALF:], query[HALF:])
            ).astype(BF16)
        return 0

    lax.fori_loop(0, PAIRS, scores_of, 0)

    def project_pair(n, slots, first, count, begin, end):
        cols = pl.ds(pl.multiple_of(n * 256, 256), 256)
        rows = pl.ds(first, count)
        total = None if begin else pacc[n, rows, :]
        for d in slots:
            part = nt(gath[d, rows, :], w4[d, cols, :])
            total = part if total is None else total + part
        if end:
            low = total.astype(BF16)
            dout[2 * n, rows, :] = low[:, :128]
            dout[2 * n + 1, rows, :] = low[:, 128:]
        else:
            pacc[n, rows, :] = total

    def project(*how):
        for n in range(PAIRS):
            project_pair(n, *how)

    def scaled_queries(p, e, first):
        rows = qT[p, e * 64:(e + 1) * 64, first:first + HALF].astype(F32)
        scaled = [
            (lam[LB + 1 + b, pl.ds(2 * p + e, 1), :][:, first:first + HALF] * rows).astype(BF16)
            for b in range(SEQ_BITS)
        ]
        return jnp.concatenate(scaled, axis=0)

    def level_first(p, _):
        for e in range(2):
            lgacc[p, e] = nn(scaled_queries(p, e, 0), dout[2 * p + e, 0:HALF, :])
        return 0

    def scale_rest(p, _):
        for e in range(2):
            rest[p, e] = scaled_queries(p, e, HALF)
        return 0

    def level_last(p):
        for e in range(2):
            grads = (lgacc[p, e] + nn(rest[p, e], dout[2 * p + e, HALF:ROWS, :])).astype(BF16)
            at = pl.ds(pl.multiple_of(p * 128 + e * 64, 64), 64)
            for b in range(SEQ_BITS):
                lg[b, at, :] = grads[b * 64:(b + 1) * 64, :]

    for load in loads[14:]:
        load.wait()
    project([y], 0, ROWS, True, False)
    arrive(s1[0])
    start(s1[1])
    turn(0)
    arrive(s1[1])
    start(s1[2])
    turn(1)
    project([left, right], 0, HALF, False, False)
    arrive(s1[2])
    start(s1[3])
    turn(2)

    arrive(s1[3])
    parts = [zbuf[flipped(z, i, 3)].astype(F32) for i in range(8)]
    pair1 = parts[2] + parts[3]
    quad = (parts[4] + parts[5]) + (parts[6] + parts[7])
    xbuf[0] = ((parts[0] + parts[1]) + pair1 + quad).astype(BF16)
    s2 = start([remote(xbuf.at[0], xbuf.at[i], ss, sr, S2 + i - 1, x_peer(i)) for i in (1, 3)])
    state_low[1, mine, :] = parts[1].astype(BF16)
    state_low[2, mine, :] = pair1.astype(BF16)
    state_low[3, mine, :] = quad.astype(BF16)

    turn(3)
    arrive(s2)
    s2 = start([remote(xbuf.at[1], xbuf.at[2], ss, sr, S2 + 1, x_peer(3))])
    project([left, right], HALF, HALF, False, False)
    lax.fori_loop(0, PAIRS, scale_rest, 0)
    arrive(forwards[0])
    arrive(forwards[1])
    project([across], 0, HALF, False, True)
    lax.fori_loop(0, PAIRS, level_first, 0, unroll=True)

    arrive(forwards[2])
    project([across], HALF, CROWS, False, True)
    arrive(forwards[3])
    project([across], HALF + CROWS, CROWS, False, True)

    r0 = [[], []]
    for i in range(2):
        p = 2 * (1 - c) + i
        level_last(p)
        rows = pl.ds(pl.multiple_of(p * 128, 128), 128)
        for b in (3, 4, 0, 1, 2):
            r0[b // 3] += start([
                remote(lg.at[1 + b, rows], rbh.at[b, pl.ds(i * 128, 128)], ss, sr, R0 + 5 * i + b, partner)
            ])
    for i in range(2):
        level_last(2 * c + i)

    def owned(at):
        return pl.ds(pl.multiple_of(at * SLICE, SLICE), SLICE)

    def chip_sum(first, count):
        levels = pl.ds(first, count)
        rsrc[levels] = (lg[pl.ds(1 + first, count), mine, :].astype(F32) + rbh[levels].astype(F32)).astype(BF16)

    def slice_of(i, level):
        return remote(rsrc.at[level, owned(flipped(z, i, 3))], rbuf.at[i, level], ss, sr, R1 + level, z_peer(i))

    def slices(count, level):
        some = rbuf.at[pl.ds(1, count), level]
        return remote(some, some, ss, sr, R1 + level, z_peer(1))

    set_bits = [(z // 2**b) % 2 for b in range(3)] + [x % 2, x // 2]

    def send_level(i, level):
        @pl.when(set_bits[level] == 1)
        def _():
            slice_of(i, level).start()

    arrive(r0[1])
    chip_sum(3, 2)
    for i in FAR_FIRST:
        for level in (3, 4):
            send_level(i, level)
    arrive(r0[0])
    chip_sum(0, 3)
    for i in FAR_FIRST:
        for level in range(3):
            send_level(i, level)
    rbuf[0] = rsrc[:, owned(z), :]
    rb = start([remote(lg.at[0], rb0, ss, sr, R0 + 10, partner)])
    arrive(s2)
    state_low[4, mine, :] = xbuf[1]
    state_low[5, mine, :] = (xbuf[2].astype(F32) + xbuf[3].astype(F32)).astype(BF16)
    s4 = start([
        remote(state_low.at[b, mine], state_low.at[b, mine], ss, sr, S4 + b - 1, partner) for b in range(1, SEQ_BITS)
    ])
    arrive(s4)

    def attention(p, _):
        turned_k = kT[p]
        values = vp[p]
        query = qp[p]
        lines = []
        for e in range(2):
            h = 2 * p + e
            mine_q = masked(query, e)
            d = dout[h]
            mine_v = values[:, e * 128:(e + 1) * 128]
            low = (mix_of(h, 0, HALF, 0, ROWS) * nt(mine_v[:HALF], d)).astype(BF16)
            high = (mix_of(h, HALF, HALF, HALF, HALF) * nt(mine_v[HALF:], d[HALF:])).astype(BF16)
            key_low = nn(low, mine_q)
            key_high = nn(high, mine_q[HALF:])
            if e == 0:
                kacc[p, pl.ds(0, HALF), :] = key_low
                kacc[p, pl.ds(HALF, HALF), :] = key_high
            else:
                kacc[p, pl.ds(0, HALF), :] += key_low
                kacc[p, pl.ds(HALF, HALF), :] += key_high
            vacc[p, pl.ds(0, HALF), pl.ds(e * 128, 128)] = nn(sm[h, pl.ds(0, HALF), :], d)
            vacc[p, pl.ds(HALF, HALF), pl.ds(e * 128, 128)] = nn(
                sm[h, pl.ds(HALF, HALF), pl.ds(HALF, HALF)], d[HALF:]
            )
            own_k = turned_k[e * 64:(e + 1) * 64, :]
            line = nn(own_k[:, :HALF], low)
            line_high = nn(own_k[:, HALF:], high)
            at = pl.ds(pl.multiple_of(h * 64, 64), 64)
            states = state_low[:, at, :].reshape(SEQ_BITS * 64, 128)
            read = nt(states, d)
            for b in range(SEQ_BITS):
                line = line + lam[LB + 1 + b, pl.ds(h, 1), :] * read[b * 64:(b + 1) * 64, :]
            lines.append(jnp.concatenate([line[:, :HALF], line[:, HALF:] + line_high], axis=1))
        qo[p] = jnp.concatenate(lines, axis=0).T.astype(BF16)
        return 0

    lax.fori_loop(0, 2, attention, 0)
    for copy in sent:
        copy.wait_send()
    sent.clear()
    for level in (3, 4):
        @pl.when(set_bits[level] == 1)
        def _(level=level):
            slices(7, level).wait_recv()
    tops = rbuf[0, pl.ds(3, 2)].astype(F32)
    for i in range(1, 8):
        tops = tops + rbuf[i, pl.ds(3, 2)].astype(F32)
    tsrc[...] = tops.astype(BF16)
    near = [remote(tsrc.at[0], tbuf.at[1, 0], ss, sr, R2, x_peer(1))]
    far = [remote(tsrc.at[1], tbuf.at[i, 1], ss, sr, R2 + i - 1, x_peer(i)) for i in (2, 3)]
    start_if(x // 2 == 1, far)
    start_if(x % 2 == 1, near)

    lax.fori_loop(2, 4, attention, 0)
    for level in range(3):
        @pl.when(set_bits[level] == 1)
        def _(level=level):
            slices(3, level).wait_recv()

        @pl.when(set_bits[level] == 0)
        def _(level=level):
            slices(4, level).wait_recv()
    arrive_if(x % 2 == 0, near)
    arrive_if(x // 2 == 0, far)
    outer = tbuf[1, 0].astype(F32) + tbuf[2, 1].astype(F32) + tbuf[3, 1].astype(F32)
    finals = pl.ds(pl.multiple_of(c * HALF + z * SLICE, SLICE), SLICE)
    for r in FAR_FIRST + (0,):
        total = outer
        for i in range(1, 8):
            total = total + rbuf[r ^ i, i.bit_length() - 1].astype(F32)
        rets[r] = total.astype(BF16)
        if r:
            remote(rets.at[r], rfin.at[finals], ss, sr, R3, z_peer(r)).start()
        remote(rets.at[r], rfin.at[finals], ss, sr, R3, z_other(r) if r else partner).start()
    rfin[finals, :] = rets[0]
    for copy in sent:
        copy.wait_send()
    for level in range(5):
        @pl.when(set_bits[level] == 1)
        def _(level=level):
            slices(7, level).wait_send()
    for condition, copies in sent_if:
        @pl.when(condition)
        def _(copies=copies):
            for copy in copies:
                copy.wait_send()
    arrive(rb)
    every = rfin.at[pl.ds(0, 15 * SLICE)]
    last = remote(every, every, ss, sr, R3, partner)
    last.wait_recv()
    ret_ref[...] = (rfin[...].astype(F32) + rb0[...].astype(F32)).astype(BF16)
    last.wait_send()


def finish(back_ref, k_ref, v_ref, q_ref, kacc_ref, vacc_ref, qo_hbm, ko_hbm, vo_hbm, ko, vo, sem):
    copies = []

    def send(src, dst):
        copies.append(pltpu.make_async_copy(src, dst, sem.at[len(copies)]))
        copies[-1].start()

    for p in range(PAIRS):
        send(q_ref.at[p], qo_hbm.at[:, pl.ds(p * 128, 128)])
    zero = jnp.zeros((64, 128), BF16)
    for p in range(PAIRS):
        back = back_ref[pl.ds(p * 128, 128), :]
        spread = jnp.concatenate([
            jnp.concatenate([back[:64], zero], axis=1),
            jnp.concatenate([zero, back[64:]], axis=1),
        ], axis=0)
        vo[p] = (vacc_ref[p] + nn(k_ref[p], spread)).astype(BF16)
        send(vo.at[p], vo_hbm.at[:, pl.ds(p * 256, 256)])
        ko[p] = (kacc_ref[p] + nt(v_ref[p], spread)).astype(BF16)
        send(ko.at[p], ko_hbm.at[:, pl.ds(p * 128, 128)])
    for copy in copies:
        copy.wait()


def per_device(query_rows, key_rows, value_rows, out_grad, out_weight, level_codes, level_table):
    any_space = pl.BlockSpec(memory_space=pl.ANY)
    vmem = pl.BlockSpec(memory_space=pltpu.VMEM)
    scratch = [
        pltpu.VMEM((PAIRS, ROWS, 128), BF16),
        pltpu.VMEM((4, HEADS * DV, FEAT), BF16),
        pltpu.VMEM((4, ROWS, FEAT), BF16),
        pltpu.VMEM((HEADS, ROWS, DV), BF16),
        pltpu.VMEM((PAIRS, 128, ROWS), BF16),
        pltpu.VMEM((PAIRS, 128, ROWS), BF16),
        pltpu.VMEM((LB + 1 + SEQ_BITS, HEADS, ROWS), F32),
        pltpu.VMEM((ROWS // BLK, HEADS, ROWS), F32),
        pltpu.VMEM((HEADS, ROWS, ROWS), BF16),
        pltpu.VMEM((ROWS, 128), F32),
        pltpu.VMEM((ROWS, 128), F32),
        pltpu.VMEM((8, HALF, 128), BF16),
        pltpu.VMEM((4, HALF, 128), BF16),
        pltpu.VMEM((SEQ_BITS, ROWS, 128), BF16),
        pltpu.VMEM((SEQ_BITS, ROWS, 128), BF16),
        pltpu.VMEM((ROWS, 128), BF16),
        pltpu.VMEM((5, HALF, 128), BF16),
        pltpu.VMEM((5, HALF, 128), BF16),
        pltpu.VMEM((8, 5, SLICE, 128), BF16),
        pltpu.VMEM((2, SLICE, 128), BF16),
        pltpu.VMEM((4, 2, SLICE, 128), BF16),
        pltpu.VMEM((8, SLICE, 128), BF16),
        pltpu.VMEM((ROWS, 128), BF16),
        pltpu.VMEM((4, ROWS, 256), F32),
        pltpu.VMEM((PAIRS, 2, SEQ_BITS * 64, 128), F32),
        pltpu.VMEM((PAIRS, 2, SEQ_BITS * 64, HALF), BF16),
        pltpu.VMEM((12, HEADS, ROWS), jnp.int32),
        pltpu.VMEM((HEADS, 16), F32),
        pltpu.SemaphoreType.DMA((19,)),
        pltpu.SemaphoreType.DMA((16,)),
        pltpu.SemaphoreType.DMA((16,)),
        pltpu.SemaphoreType.DMA((N_SEM,)),
        pltpu.SemaphoreType.DMA((N_SEM,)),
    ]
    inputs = [
        pltpu.with_memory_space_constraint(array, pltpu.HBM)
        for array in (query_rows, key_rows, value_rows, out_grad, out_weight, level_codes, level_table)
    ]
    queries, keys, values, returned, key_pairs, value_pairs = pl.pallas_call(
        kernel,
        out_shape=(
            pltpu.VMEM((PAIRS, ROWS, 128), BF16),
            pltpu.VMEM((PAIRS, ROWS, 128), F32),
            pltpu.VMEM((PAIRS, ROWS, 256), F32),
            pltpu.VMEM((ROWS, 128), BF16),
            pltpu.VMEM((PAIRS, ROWS, 128), BF16),
            pltpu.VMEM((PAIRS, ROWS, 256), BF16),
        ),
        in_specs=[any_space] * 7,
        out_specs=(vmem,) * 6,
        scratch_shapes=scratch,
        compiler_params=pltpu.CompilerParams(
            collective_id=0, has_side_effects=True, vmem_limit_bytes=40 * 1024 * 1024
        ),
        cost_estimate=pl.CostEstimate(flops=8_000_000_000, bytes_accessed=12_000_000, transcendentals=0),
    )(*inputs)
    return pl.pallas_call(
        finish,
        out_shape=(
            jax.ShapeDtypeStruct((ROWS, HEADS * DK), BF16),
            jax.ShapeDtypeStruct((ROWS, HEADS * DK), BF16),
            jax.ShapeDtypeStruct((ROWS, HEADS * DV), BF16),
        ),
        in_specs=[vmem] * 6,
        out_specs=(any_space,) * 3,
        scratch_shapes=[
            pltpu.VMEM((PAIRS, ROWS, 128), BF16),
            pltpu.VMEM((PAIRS, ROWS, 256), BF16),
            pltpu.SemaphoreType.DMA((3 * PAIRS,)),
        ],
        compiler_params=pltpu.CompilerParams(vmem_limit_bytes=16 * 1024 * 1024),
        cost_estimate=pl.CostEstimate(flops=500_000_000, bytes_accessed=8_000_000, transcendentals=0),
    )(returned, key_pairs, value_pairs, queries, keys, values)


def solution(mesh):
    return jax.shard_map(
        per_device,
        mesh=mesh,
        in_specs=(
            P("seq", "head"),
            P("seq", "head"),
            P("seq", "head"),
            P("seq", "head"),
            P("head", None),
            P(None, "head", "seq"),
            P("head", None),
        ),
        out_specs=(P("seq", "head"), P("seq", "head"), P("seq", "head")),
        check_vma=False,
    )
```

```python
import jax
import jax.numpy as jnp
from jax import lax
from jax.experimental import pallas as pl
from jax.experimental.pallas import tpu as pltpu
from jax.sharding import PartitionSpec as P

DK = 64
DV = 128
BLK = 64
LB = 3
SEQ_BITS = 6
ROWS = 512
HEADS = 8
PAIRS = 4
FEAT = 768
CHUNKS = 4
CROWS = ROWS // CHUNKS
HALF = 256
SLICE = 32
SCALES = [float((DK * BLK * 2 ** max(level - 1, 0)) ** -0.5) for level in range(LB + 1 + SEQ_BITS)]

F32 = jnp.float32
BF16 = jnp.bfloat16

S0, S1, S2, S4, R0, R1, R2, R3, N_SEM = 0, 1, 8, 11, 16, 27, 32, 35, 36
FAR_FIRST = (4, 5, 3, 7, 6, 2, 1)


def nt(a, b):
    return lax.dot_general(a, b, (((1,), (1,)), ((), ())), preferred_element_type=F32)


def nn(a, b):
    return lax.dot_general(a, b, (((1,), (0,)), ((), ())), preferred_element_type=F32)


def flipped(value, mask, bits):
    out = value
    for k in range(bits):
        if mask >> k & 1:
            out = out + (1 - 2 * ((value // 2**k) % 2)) * 2**k
    return out


def kernel(
    q_hbm, k_hbm, v_hbm, og_hbm, w_hbm, codes_hbm, table_hbm,
    qo, kacc, vacc, ret_ref, kp, vp,
    qp, w4, gath, dout, kT, qT, lam, inner, sm,
    gsb, pgs, zbuf, xbuf, state_low,
    lg, rb0, rbh, rsrc, rbuf, tsrc, tbuf, rets, rfin,
    pacc, lgacc, rest, qacc, w_turned, codes_ref, table_ref,
    loc_sem, ys, yr, ss, sr,
):
    g = lax.axis_index("seq")
    y = lax.axis_index("head")
    c = g % 2
    z = (g // 2) % 8
    x = g // 16
    right, left, across = (y + 1) % 4, (y + 3) % 4, (y + 2) % 4

    def z_peer(i):
        return (x * 16 + flipped(z, i, 3) * 2 + c, y)

    def z_other(i):
        return (x * 16 + flipped(z, i, 3) * 2 + 1 - c, y)

    def x_peer(i):
        return (flipped(x, i, 2) * 16 + z * 2 + c, y)

    partner = (g + 1 - 2 * c, y)
    def z_ring(step):
        return (x * 16 + ((z + step) % 8) * 2 + c, y)

    peers = [partner, (g, right), (g, left), z_ring(1), z_ring(7), x_peer(1), x_peer(3)]

    barrier = pltpu.get_barrier_semaphore()
    for peer in peers:
        pl.semaphore_signal(barrier, inc=1, device_id=peer, device_id_type=pl.DeviceIdType.MESH)

    loads = []
    for p in range(PAIRS):
        loads.append(pltpu.make_async_copy(k_hbm.at[:, pl.ds(p * 128, 128)], kp.at[p], loc_sem.at[len(loads)]))
    for p in range(PAIRS):
        loads.append(pltpu.make_async_copy(v_hbm.at[:, pl.ds(p * 256, 256)], vp.at[p], loc_sem.at[len(loads)]))
    for p in range(PAIRS):
        loads.append(pltpu.make_async_copy(q_hbm.at[:, pl.ds(p * 128, 128)], qp.at[p], loc_sem.at[len(loads)]))
    loads.append(pltpu.make_async_copy(codes_hbm, codes_ref, loc_sem.at[len(loads)]))
    loads.append(pltpu.make_async_copy(table_hbm, table_ref, loc_sem.at[len(loads)]))
    loads.append(pltpu.make_async_copy(og_hbm, gath.at[y], loc_sem.at[len(loads)]))
    for p in range(4):
        loads.append(pltpu.make_async_copy(w_hbm.at[:, pl.ds(p * FEAT, FEAT)], w4.at[p], loc_sem.at[len(loads)]))
    pl.semaphore_wait(barrier, len(peers))

    def remote(src, dst, send, recv, slot, to):
        return pltpu.make_async_remote_copy(
            src_ref=src, dst_ref=dst, send_sem=send.at[slot], recv_sem=recv.at[slot],
            device_id=to, device_id_type=pl.DeviceIdType.MESH,
        )

    def own(j):
        rows = pl.ds(j * CROWS, CROWS)
        return [
            remote(og_hbm.at[rows], gath.at[y, rows], ys, yr, j, (g, right)),
            remote(og_hbm.at[rows], gath.at[y, rows], ys, yr, 4 + j, (g, left)),
        ]

    def forward(j):
        first = pl.ds(j * CROWS, CROWS // 2)
        second = pl.ds(j * CROWS + CROWS // 2, CROWS // 2)
        return [
            remote(gath.at[left, first], gath.at[left, first], ys, yr, 8 + j, (g, right)),
            remote(gath.at[right, second], gath.at[right, second], ys, yr, 12 + j, (g, left)),
        ]

    def start(copies):
        for copy in copies:
            copy.start()
        sent.extend(copies)
        return copies

    def arrive(copies):
        for copy in copies:
            copy.wait_recv()

    def start_if(condition, copies):
        @pl.when(condition)
        def _():
            for copy in copies:
                copy.start()

        sent_if.append((condition, copies))

    def arrive_if(condition, copies):
        @pl.when(condition)
        def _():
            arrive(copies)

    sent, sent_if = [], []
    owns = [own(j) for j in range(CHUNKS)]
    forwards = [forward(j) for j in range(CHUNKS)]
    for j in range(CHUNKS):
        start(owns[j])
    for load in loads:
        load.start()
    rbuf[...] = jnp.zeros_like(rbuf)
    tbuf[...] = jnp.zeros_like(tbuf)
    for load in loads[:8]:
        load.wait()

    def states_of(p, _):
        kT[p] = kp[p].T
        both = nn(kT[p], vp[p])
        at = pl.multiple_of(p * 128, 128)
        gsb[pl.ds(at, 64), :] = both[:64, :128]
        gsb[pl.ds(at + 64, 64), :] = both[64:, 128:]
        return 0

    lax.fori_loop(0, PAIRS, states_of, 0)
    s0 = start([remote(gsb, pgs, ss, sr, S0, partner)])

    for load in loads[8:14]:
        load.wait()
    table = table_ref[...]
    columns = [jnp.broadcast_to(table[:, j:j + 1], (HEADS, ROWS)) for j in range(16)]
    for level in range(LB + 1 + SEQ_BITS):
        codes = codes_ref[level]
        looked = jnp.zeros((HEADS, ROWS), F32)
        for j in range(16):
            looked = jnp.where(codes == j, columns[j], looked)
        looked = looked * SCALES[level]
        if level > LB:
            looked = looked * ((g // 2 ** (level - LB - 1)) % 2).astype(F32)
        lam[level] = looked
    token_block = lax.broadcasted_iota(jnp.int32, (HEADS, ROWS), 1) // BLK
    for cs in range(ROWS // BLK):
        line = jnp.zeros((HEADS, ROWS), F32)
        for ct in range(cs, ROWS // BLK):
            line = jnp.where(token_block == ct, lam[(ct ^ cs).bit_length()], line)
        inner[cs] = line

    def turned(p, _):
        qT[p] = qp[p].T
        return 0

    lax.fori_loop(0, PAIRS, turned, 0)

    mine = pl.ds(pl.multiple_of(c * HALF, HALF), HALF)
    other = pl.ds(pl.multiple_of((1 - c) * HALF, HALF), HALF)
    arrive(s0)
    zbuf[z] = (gsb[mine, :] + pgs[mine, :]).astype(BF16)

    def ring(k):
        ahead, back = zbuf.at[(z + 8 - k) % 8], zbuf.at[(z + k) % 8]
        copies = [remote(ahead, ahead, ss, sr, S1 + k, z_ring(1))]
        if k < 3:
            copies.append(remote(back, back, ss, sr, S1 + 4 + k, z_ring(7)))
        return copies

    s1 = [ring(k) for k in range(4)]
    start(s1[0])
    state_low[0] = pgs[...].astype(BF16)

    def turn(j):
        arrive(owns[j])
        start(forwards[j])

    def mix_of(h, s0_, count, t0_, width):
        lines = [
            jnp.broadcast_to(inner[s0_ // BLK + i, pl.ds(h, 1), pl.ds(t0_, width)], (BLK, width))
            for i in range(count // BLK)
        ]
        mix = jnp.concatenate(lines, axis=0)
        s_at = lax.broadcasted_iota(jnp.int32, (count, width), 0) + s0_
        t_at = lax.broadcasted_iota(jnp.int32, (count, width), 1) + t0_
        return jnp.where(s_at <= t_at, mix, 0.0)

    def masked(pair, e):
        lane = lax.broadcasted_iota(jnp.int32, pair.shape, 1)
        return jnp.where((lane >= 64) == (e == 1), pair, jnp.zeros_like(pair))

    def scores_of(p, _):
        for e in range(2):
            h = 2 * p + e
            keys = masked(kp[p], e)
            query = qp[p]
            sm[h, pl.ds(0, HALF), :] = (mix_of(h, 0, HALF, 0, ROWS) * nt(keys[:HALF], query)).astype(BF16)
            sm[h, pl.ds(HALF, HALF), pl.ds(HALF, HALF)] = (
                mix_of(h, HALF, HALF, HALF, HALF) * nt(keys[HALF:], query[HALF:])
            ).astype(BF16)
        return 0

    lax.fori_loop(0, PAIRS, scores_of, 0)

    def project_pair(n, slots, first, count, begin, end):
        cols = pl.ds(pl.multiple_of(n * 256, 256), 256)
        rows = pl.ds(first, count)
        total = None if begin else pacc[n, rows, :]
        for d in slots:
            if end:
                part = nn(gath[d, rows, :], w_turned[:, cols])
            else:
                part = nt(gath[d, rows, :], w4[d, cols, :])
            total = part if total is None else total + part
        if end:
            low = total.astype(BF16)
            dout[2 * n, rows, :] = low[:, :128]
            dout[2 * n + 1, rows, :] = low[:, 128:]
        else:
            pacc[n, rows, :] = total

    def project(*how):
        for n in range(PAIRS):
            project_pair(n, *how)

    def scaled_queries(p, e, first):
        rows = qT[p, e * 64:(e + 1) * 64, first:first + HALF].astype(F32)
        scaled = [
            (lam[LB + 1 + b, pl.ds(2 * p + e, 1), :][:, first:first + HALF] * rows).astype(BF16)
            for b in range(SEQ_BITS)
        ]
        return jnp.concatenate(scaled, axis=0)

    def level_first(p, _):
        for e in range(2):
            lgacc[p, e] = nn(scaled_queries(p, e, 0), dout[2 * p + e, 0:HALF, :])
        return 0

    def scale_rest(p, _):
        for e in range(2):
            rest[p, e] = scaled_queries(p, e, HALF)
        return 0

    def level_last(p):
        for e in range(2):
            grads = (lgacc[p, e] + nn(rest[p, e], dout[2 * p + e, HALF:ROWS, :])).astype(BF16)
            at = pl.ds(pl.multiple_of(p * 128 + e * 64, 64), 64)
            for b in range(SEQ_BITS):
                lg[b, at, :] = grads[b * 64:(b + 1) * 64, :]

    for load in loads[14:]:
        load.wait()
    project([y], 0, ROWS, True, False)
    arrive(s1[0])
    start(s1[1])
    turn(0)
    arrive(s1[1])
    start(s1[2])
    turn(1)
    project([left, right], 0, HALF, False, False)
    arrive(s1[2])
    start(s1[3])
    turn(2)

    turn(3)
    arrive(s1[3])
    parts = [zbuf[flipped(z, i, 3)].astype(F32) for i in range(8)]
    pair1 = parts[2] + parts[3]
    quad = (parts[4] + parts[5]) + (parts[6] + parts[7])
    xbuf[0] = ((parts[0] + parts[1]) + pair1 + quad).astype(BF16)
    s2 = start([remote(xbuf.at[0], xbuf.at[i], ss, sr, S2 + i - 1, x_peer(i)) for i in (1, 3)])
    state_low[1, mine, :] = parts[1].astype(BF16)
    state_low[2, mine, :] = pair1.astype(BF16)
    state_low[3, mine, :] = quad.astype(BF16)

    arrive(s2)
    s2 = start([remote(xbuf.at[1], xbuf.at[2], ss, sr, S2 + 1, x_peer(3))])
    project([left, right], HALF, HALF, False, False)
    lax.fori_loop(0, PAIRS, scale_rest, 0)
    for n in range(PAIRS):
        w_turned[:, n * 256:(n + 1) * 256] = w4[across, n * 256:(n + 1) * 256, :].T
    arrive(forwards[0])
    arrive(forwards[1])
    project([across], 0, HALF, False, True)
    lax.fori_loop(0, PAIRS, level_first, 0, unroll=True)

    arrive(forwards[2])
    project([across], HALF, CROWS, False, True)
    arrive(forwards[3])
    project([across], HALF + CROWS, CROWS, False, True)

    r0 = [[], []]

    def swap(i, levels):
        rows = pl.ds(pl.multiple_of((2 * (1 - c) + i) * 128, 128), 128)
        return start([
            remote(lg.at[1 + b, rows], rbh.at[b, pl.ds(i * 128, 128)], ss, sr, R0 + 5 * i + b, partner)
            for b in levels
        ])

    for i in range(2):
        level_last(2 * (1 - c) + i)
        r0[1] += swap(i, (4, 3))
    for i in range(2):
        r0[0] += swap(i, (0, 1, 2))
    for i in range(2):
        level_last(2 * c + i)

    def owned(at):
        return pl.ds(pl.multiple_of(at * SLICE, SLICE), SLICE)

    def chip_sum(first, count):
        levels = pl.ds(first, count)
        rsrc[levels] = (lg[pl.ds(1 + first, count), mine, :].astype(F32) + rbh[levels].astype(F32)).astype(BF16)

    def slice_of(i, level):
        return remote(rsrc.at[level, owned(flipped(z, i, 3))], rbuf.at[i, level], ss, sr, R1 + level, z_peer(i))

    def slices(count, level):
        some = rbuf.at[pl.ds(1, count), level]
        return remote(some, some, ss, sr, R1 + level, z_peer(1))

    set_bits = [(z // 2**b) % 2 for b in range(3)] + [x % 2, x // 2]

    def send_level(i, level):
        @pl.when(set_bits[level] == 1)
        def _():
            slice_of(i, level).start()

    arrive(r0[1])
    chip_sum(3, 2)
    for level in (4, 3):
        for i in FAR_FIRST:
            send_level(i, level)
    arrive(r0[0])
    chip_sum(0, 3)
    for i in FAR_FIRST:
        for level in range(3):
            send_level(i, level)
    rbuf[0] = rsrc[:, owned(z), :]
    rb = start([remote(lg.at[0], rb0, ss, sr, R0 + 10, partner)])
    def attention(p, _):
        turned_k = kT[p]
        values = vp[p]
        query = qp[p]
        for e in range(2):
            h = 2 * p + e
            mine_q = masked(query, e)
            d = dout[h]
            mine_v = values[:, e * 128:(e + 1) * 128]
            low = (mix_of(h, 0, HALF, 0, ROWS) * nt(mine_v[:HALF], d)).astype(BF16)
            high = (mix_of(h, HALF, HALF, HALF, HALF) * nt(mine_v[HALF:], d[HALF:])).astype(BF16)
            key_low = nn(low, mine_q)
            key_high = nn(high, mine_q[HALF:])
            if e == 0:
                kacc[p, pl.ds(0, HALF), :] = key_low
                kacc[p, pl.ds(HALF, HALF), :] = key_high
            else:
                kacc[p, pl.ds(0, HALF), :] += key_low
                kacc[p, pl.ds(HALF, HALF), :] += key_high
            vacc[p, pl.ds(0, HALF), pl.ds(e * 128, 128)] = nn(sm[h, pl.ds(0, HALF), :], d)
            vacc[p, pl.ds(HALF, HALF), pl.ds(e * 128, 128)] = nn(
                sm[h, pl.ds(HALF, HALF), pl.ds(HALF, HALF)], d[HALF:]
            )
            own_k = turned_k[e * 64:(e + 1) * 64, :]
            line = nn(own_k[:, :HALF], low)
            line_high = nn(own_k[:, HALF:], high)
            qacc[p, pl.ds(e * 64, 64), :] = jnp.concatenate([line[:, :HALF], line[:, HALF:] + line_high], axis=1)
        return 0

    def read_states(p, _):
        lines = []
        for e in range(2):
            h = 2 * p + e
            at = pl.ds(pl.multiple_of(h * 64, 64), 64)
            read = nt(state_low[:, at, :].reshape(SEQ_BITS * 64, 128), dout[h])
            line = qacc[p, pl.ds(e * 64, 64), :]
            for b in range(SEQ_BITS):
                line = line + lam[LB + 1 + b, pl.ds(h, 1), :] * read[b * 64:(b + 1) * 64, :]
            lines.append(line)
        qo[p] = jnp.concatenate(lines, axis=0).T.astype(BF16)
        return 0

    lax.fori_loop(0, 2, attention, 0)
    for copy in sent:
        copy.wait_send()
    sent.clear()
    near = [remote(tsrc.at[0], tbuf.at[1, 0], ss, sr, R2, x_peer(1))]
    far = [remote(tsrc.at[1], tbuf.at[i, 1], ss, sr, R2 + i - 1, x_peer(i)) for i in (2, 3)]
    arrive(s2)
    for level, copies in ((4, far), (3, near)):
        @pl.when(set_bits[level] == 1)
        def _(level=level):
            slices(7, level).wait_recv()

        top = rbuf[0, level].astype(F32)
        for i in range(1, 8):
            top = top + rbuf[i, level].astype(F32)
        tsrc[level - 3] = top.astype(BF16)
        start_if(set_bits[level] == 1, copies)

    state_low[4, mine, :] = xbuf[1]
    state_low[5, mine, :] = (xbuf[2].astype(F32) + xbuf[3].astype(F32)).astype(BF16)
    s4 = start([
        remote(state_low.at[b, mine], state_low.at[b, mine], ss, sr, S4 + b - 1, partner) for b in range(1, SEQ_BITS)
    ])
    lax.fori_loop(2, 4, attention, 0)
    for level in range(3):
        @pl.when(set_bits[level] == 1)
        def _(level=level):
            slices(3, level).wait_recv()

        @pl.when(set_bits[level] == 0)
        def _(level=level):
            slices(4, level).wait_recv()
    arrive_if(x % 2 == 0, near)
    arrive_if(x // 2 == 0, far)
    outer = tbuf[1, 0].astype(F32) + tbuf[2, 1].astype(F32) + tbuf[3, 1].astype(F32)
    finals = pl.ds(pl.multiple_of(c * HALF + z * SLICE, SLICE), SLICE)
    for r in FAR_FIRST + (0,):
        total = outer
        for i in range(1, 8):
            total = total + rbuf[r ^ i, i.bit_length() - 1].astype(F32)
        rets[r] = total.astype(BF16)
        if r:
            remote(rets.at[r], rfin.at[finals], ss, sr, R3, z_peer(r)).start()
        remote(rets.at[r], rfin.at[finals], ss, sr, R3, z_other(r) if r else partner).start()
    rfin[finals, :] = rets[0]
    arrive(s4)
    lax.fori_loop(0, PAIRS, read_states, 0)
    for copy in sent:
        copy.wait_send()
    for level in range(5):
        @pl.when(set_bits[level] == 1)
        def _(level=level):
            slices(7, level).wait_send()
    for condition, copies in sent_if:
        @pl.when(condition)
        def _(copies=copies):
            for copy in copies:
                copy.wait_send()
    arrive(rb)
    every = rfin.at[pl.ds(0, 15 * SLICE)]
    last = remote(every, every, ss, sr, R3, partner)
    last.wait_recv()
    ret_ref[...] = (rfin[...].astype(F32) + rb0[...].astype(F32)).astype(BF16)
    last.wait_send()


def finish(back_ref, k_ref, v_ref, q_ref, kacc_ref, vacc_ref, qo_hbm, ko_hbm, vo_hbm, ko, vo, sem):
    copies = []

    def send(src, dst):
        copies.append(pltpu.make_async_copy(src, dst, sem.at[len(copies)]))
        copies[-1].start()

    for p in range(PAIRS):
        send(q_ref.at[p], qo_hbm.at[:, pl.ds(p * 128, 128)])
    zero = jnp.zeros((64, 128), BF16)
    for p in range(PAIRS):
        back = back_ref[pl.ds(p * 128, 128), :]
        spread = jnp.concatenate([
            jnp.concatenate([back[:64], zero], axis=1),
            jnp.concatenate([zero, back[64:]], axis=1),
        ], axis=0)
        vo[p] = (vacc_ref[p] + nn(k_ref[p], spread)).astype(BF16)
        send(vo.at[p], vo_hbm.at[:, pl.ds(p * 256, 256)])
        ko[p] = (kacc_ref[p] + nt(v_ref[p], spread)).astype(BF16)
        send(ko.at[p], ko_hbm.at[:, pl.ds(p * 128, 128)])
    for copy in copies:
        copy.wait()


def per_device(query_rows, key_rows, value_rows, out_grad, out_weight, level_codes, level_table):
    any_space = pl.BlockSpec(memory_space=pl.ANY)
    vmem = pl.BlockSpec(memory_space=pltpu.VMEM)
    scratch = [
        pltpu.VMEM((PAIRS, ROWS, 128), BF16),
        pltpu.VMEM((4, HEADS * DV, FEAT), BF16),
        pltpu.VMEM((4, ROWS, FEAT), BF16),
        pltpu.VMEM((HEADS, ROWS, DV), BF16),
        pltpu.VMEM((PAIRS, 128, ROWS), BF16),
        pltpu.VMEM((PAIRS, 128, ROWS), BF16),
        pltpu.VMEM((LB + 1 + SEQ_BITS, HEADS, ROWS), F32),
        pltpu.VMEM((ROWS // BLK, HEADS, ROWS), F32),
        pltpu.VMEM((HEADS, ROWS, ROWS), BF16),
        pltpu.VMEM((ROWS, 128), F32),
        pltpu.VMEM((ROWS, 128), F32),
        pltpu.VMEM((8, HALF, 128), BF16),
        pltpu.VMEM((4, HALF, 128), BF16),
        pltpu.VMEM((SEQ_BITS, ROWS, 128), BF16),
        pltpu.VMEM((SEQ_BITS, ROWS, 128), BF16),
        pltpu.VMEM((ROWS, 128), BF16),
        pltpu.VMEM((5, HALF, 128), BF16),
        pltpu.VMEM((5, HALF, 128), BF16),
        pltpu.VMEM((8, 5, SLICE, 128), BF16),
        pltpu.VMEM((2, SLICE, 128), BF16),
        pltpu.VMEM((4, 2, SLICE, 128), BF16),
        pltpu.VMEM((8, SLICE, 128), BF16),
        pltpu.VMEM((ROWS, 128), BF16),
        pltpu.VMEM((4, ROWS, 256), F32),
        pltpu.VMEM((PAIRS, 2, SEQ_BITS * 64, 128), F32),
        pltpu.VMEM((PAIRS, 2, SEQ_BITS * 64, HALF), BF16),
        pltpu.VMEM((PAIRS, 128, ROWS), F32),
        pltpu.VMEM((FEAT, HEADS * DV), BF16),
        pltpu.VMEM((12, HEADS, ROWS), jnp.int32),
        pltpu.VMEM((HEADS, 16), F32),
        pltpu.SemaphoreType.DMA((19,)),
        pltpu.SemaphoreType.DMA((16,)),
        pltpu.SemaphoreType.DMA((16,)),
        pltpu.SemaphoreType.DMA((N_SEM,)),
        pltpu.SemaphoreType.DMA((N_SEM,)),
    ]
    inputs = [
        pltpu.with_memory_space_constraint(array, pltpu.HBM)
        for array in (query_rows, key_rows, value_rows, out_grad, out_weight, level_codes, level_table)
    ]
    queries, keys, values, returned, key_pairs, value_pairs = pl.pallas_call(
        kernel,
        out_shape=(
            pltpu.VMEM((PAIRS, ROWS, 128), BF16),
            pltpu.VMEM((PAIRS, ROWS, 128), F32),
            pltpu.VMEM((PAIRS, ROWS, 256), F32),
            pltpu.VMEM((ROWS, 128), BF16),
            pltpu.VMEM((PAIRS, ROWS, 128), BF16),
            pltpu.VMEM((PAIRS, ROWS, 256), BF16),
        ),
        in_specs=[any_space] * 7,
        out_specs=(vmem,) * 6,
        scratch_shapes=scratch,
        compiler_params=pltpu.CompilerParams(
            collective_id=0, has_side_effects=True, vmem_limit_bytes=40 * 1024 * 1024
        ),
        cost_estimate=pl.CostEstimate(flops=8_000_000_000, bytes_accessed=12_000_000, transcendentals=0),
    )(*inputs)
    return pl.pallas_call(
        finish,
        out_shape=(
            jax.ShapeDtypeStruct((ROWS, HEADS * DK), BF16),
            jax.ShapeDtypeStruct((ROWS, HEADS * DK), BF16),
            jax.ShapeDtypeStruct((ROWS, HEADS * DV), BF16),
        ),
        in_specs=[vmem] * 6,
        out_specs=(any_space,) * 3,
        scratch_shapes=[
            pltpu.VMEM((PAIRS, ROWS, 128), BF16),
            pltpu.VMEM((PAIRS, ROWS, 256), BF16),
            pltpu.SemaphoreType.DMA((3 * PAIRS,)),
        ],
        compiler_params=pltpu.CompilerParams(vmem_limit_bytes=16 * 1024 * 1024),
        cost_estimate=pl.CostEstimate(flops=500_000_000, bytes_accessed=8_000_000, transcendentals=0),
    )(returned, key_pairs, value_pairs, queries, keys, values)


def solution(mesh):
    return jax.shard_map(
        per_device,
        mesh=mesh,
        in_specs=(
            P("seq", "head"),
            P("seq", "head"),
            P("seq", "head"),
            P("seq", "head"),
            P("head", None),
            P(None, "head", "seq"),
            P("head", None),
        ),
        out_specs=(P("seq", "head"), P("seq", "head"), P("seq", "head")),
        check_vma=False,
    )
```

```python
import jax
import jax.numpy as jnp
from jax import lax
from jax.experimental import pallas as pl
from jax.experimental.pallas import tpu as pltpu
from jax.sharding import PartitionSpec as P

DK = 64
DV = 128
BLK = 64
LB = 3
SEQ_BITS = 6
ROWS = 512
HEADS = 8
PAIRS = 4
FEAT = 768
CHUNKS = 4
CROWS = ROWS // CHUNKS
HALF = 256
SLICE = 32
SCALES = [float((DK * BLK * 2 ** max(level - 1, 0)) ** -0.5) for level in range(LB + 1 + SEQ_BITS)]

F32 = jnp.float32
BF16 = jnp.bfloat16

S0, S1, S2, S4, R0, R1, R2, R3, N_SEM = 0, 1, 8, 11, 16, 27, 32, 35, 36
FAR_FIRST = (4, 5, 3, 7, 6, 2, 1)


def nt(a, b):
    return lax.dot_general(a, b, (((1,), (1,)), ((), ())), preferred_element_type=F32)


def nn(a, b):
    return lax.dot_general(a, b, (((1,), (0,)), ((), ())), preferred_element_type=F32)


def flipped(value, mask, bits):
    out = value
    for k in range(bits):
        if mask >> k & 1:
            out = out + (1 - 2 * ((value // 2**k) % 2)) * 2**k
    return out


def kernel(
    q_hbm, k_hbm, v_hbm, og_hbm, w_hbm, codes_hbm, table_hbm,
    qo, kacc, vacc, ret_ref, kp, vp,
    qp, w4, gath, dout, kT, qT, lam, inner, sm,
    gsb, pgs, zbuf, xbuf, state_low,
    lg, rb0, rbh, rsrc, rbuf, tsrc, tbuf, rets, rfin,
    pacc, lgacc, rest, qacc, w_turned, codes_ref, table_ref,
    loc_sem, ys, yr, ss, sr,
):
    g = lax.axis_index("seq")
    y = lax.axis_index("head")
    c = g % 2
    z = (g // 2) % 8
    x = g // 16
    right, left, across = (y + 1) % 4, (y + 3) % 4, (y + 2) % 4

    def z_peer(i):
        return (x * 16 + flipped(z, i, 3) * 2 + c, y)

    def z_other(i):
        return (x * 16 + flipped(z, i, 3) * 2 + 1 - c, y)

    def x_peer(i):
        return (flipped(x, i, 2) * 16 + z * 2 + c, y)

    partner = (g + 1 - 2 * c, y)
    def z_ring(step):
        return (x * 16 + ((z + step) % 8) * 2 + c, y)

    peers = [partner, (g, right), (g, left), z_ring(1), z_ring(7), x_peer(1), x_peer(3)]

    barrier = pltpu.get_barrier_semaphore()
    for peer in peers:
        pl.semaphore_signal(barrier, inc=1, device_id=peer, device_id_type=pl.DeviceIdType.MESH)

    loads = []
    for p in range(PAIRS):
        loads.append(pltpu.make_async_copy(k_hbm.at[:, pl.ds(p * 128, 128)], kp.at[p], loc_sem.at[len(loads)]))
    for p in range(PAIRS):
        loads.append(pltpu.make_async_copy(v_hbm.at[:, pl.ds(p * 256, 256)], vp.at[p], loc_sem.at[len(loads)]))
    for p in range(PAIRS):
        loads.append(pltpu.make_async_copy(q_hbm.at[:, pl.ds(p * 128, 128)], qp.at[p], loc_sem.at[len(loads)]))
    loads.append(pltpu.make_async_copy(codes_hbm, codes_ref, loc_sem.at[len(loads)]))
    loads.append(pltpu.make_async_copy(table_hbm, table_ref, loc_sem.at[len(loads)]))
    loads.append(pltpu.make_async_copy(og_hbm, gath.at[y], loc_sem.at[len(loads)]))
    for p in range(4):
        loads.append(pltpu.make_async_copy(w_hbm.at[:, pl.ds(p * FEAT, FEAT)], w4.at[p], loc_sem.at[len(loads)]))
    pl.semaphore_wait(barrier, len(peers))

    def remote(src, dst, send, recv, slot, to):
        return pltpu.make_async_remote_copy(
            src_ref=src, dst_ref=dst, send_sem=send.at[slot], recv_sem=recv.at[slot],
            device_id=to, device_id_type=pl.DeviceIdType.MESH,
        )

    def own(j):
        rows = pl.ds(j * CROWS, CROWS)
        return [
            remote(og_hbm.at[rows], gath.at[y, rows], ys, yr, j, (g, right)),
            remote(og_hbm.at[rows], gath.at[y, rows], ys, yr, 4 + j, (g, left)),
        ]

    def forward(j):
        first = pl.ds(j * CROWS, CROWS // 2)
        second = pl.ds(j * CROWS + CROWS // 2, CROWS // 2)
        return [
            remote(gath.at[left, first], gath.at[left, first], ys, yr, 8 + j, (g, right)),
            remote(gath.at[right, second], gath.at[right, second], ys, yr, 12 + j, (g, left)),
        ]

    def start(copies):
        for copy in copies:
            copy.start()
        sent.extend(copies)
        return copies

    def arrive(copies):
        for copy in copies:
            copy.wait_recv()

    def start_if(condition, copies):
        @pl.when(condition)
        def _():
            for copy in copies:
                copy.start()

        sent_if.append((condition, copies))

    def arrive_if(condition, copies):
        @pl.when(condition)
        def _():
            arrive(copies)

    sent, sent_if = [], []
    owns = [own(j) for j in range(CHUNKS)]
    forwards = [forward(j) for j in range(CHUNKS)]
    for j in range(CHUNKS):
        start(owns[j])
    for load in loads:
        load.start()
    rbuf[...] = jnp.zeros_like(rbuf)
    tbuf[...] = jnp.zeros_like(tbuf)
    for load in loads[:8]:
        load.wait()

    def states_of(p, _):
        kT[p] = kp[p].T
        both = nn(kT[p], vp[p])
        at = pl.multiple_of(p * 128, 128)
        gsb[pl.ds(at, 64), :] = both[:64, :128]
        gsb[pl.ds(at + 64, 64), :] = both[64:, 128:]
        return 0

    lax.fori_loop(0, PAIRS, states_of, 0)
    s0 = start([remote(gsb, pgs, ss, sr, S0, partner)])

    for load in loads[8:14]:
        load.wait()
    table = table_ref[...]
    columns = [jnp.broadcast_to(table[:, j:j + 1], (HEADS, ROWS)) for j in range(16)]
    for level in range(LB + 1 + SEQ_BITS):
        codes = codes_ref[level]
        looked = jnp.zeros((HEADS, ROWS), F32)
        for j in range(16):
            looked = jnp.where(codes == j, columns[j], looked)
        looked = looked * SCALES[level]
        if level > LB:
            looked = looked * ((g // 2 ** (level - LB - 1)) % 2).astype(F32)
        lam[level] = looked
    token_block = lax.broadcasted_iota(jnp.int32, (HEADS, ROWS), 1) // BLK
    for cs in range(ROWS // BLK):
        line = jnp.zeros((HEADS, ROWS), F32)
        for ct in range(cs, ROWS // BLK):
            line = jnp.where(token_block == ct, lam[(ct ^ cs).bit_length()], line)
        inner[cs] = line

    def turned(p, _):
        qT[p] = qp[p].T
        return 0

    lax.fori_loop(0, PAIRS, turned, 0)

    mine = pl.ds(pl.multiple_of(c * HALF, HALF), HALF)
    other = pl.ds(pl.multiple_of((1 - c) * HALF, HALF), HALF)
    arrive(s0)
    zbuf[z] = (gsb[mine, :] + pgs[mine, :]).astype(BF16)

    def ring(k):
        ahead, back = zbuf.at[(z + 8 - k) % 8], zbuf.at[(z + k) % 8]
        copies = [remote(ahead, ahead, ss, sr, S1 + k, z_ring(1))]
        if k < 3:
            copies.append(remote(back, back, ss, sr, S1 + 4 + k, z_ring(7)))
        return copies

    s1 = [ring(k) for k in range(4)]
    start(s1[0])
    state_low[0] = pgs[...].astype(BF16)

    def turn(j):
        arrive(owns[j])
        start(forwards[j])

    def mix_of(h, s0_, count, t0_, width):
        lines = [
            jnp.broadcast_to(inner[s0_ // BLK + i, pl.ds(h, 1), pl.ds(t0_, width)], (BLK, width))
            for i in range(count // BLK)
        ]
        mix = jnp.concatenate(lines, axis=0)
        s_at = lax.broadcasted_iota(jnp.int32, (count, width), 0) + s0_
        t_at = lax.broadcasted_iota(jnp.int32, (count, width), 1) + t0_
        return jnp.where(s_at <= t_at, mix, 0.0)

    def masked(pair, e):
        lane = lax.broadcasted_iota(jnp.int32, pair.shape, 1)
        return jnp.where((lane >= 64) == (e == 1), pair, jnp.zeros_like(pair))

    def scores_of(p, _):
        for e in range(2):
            h = 2 * p + e
            keys = masked(kp[p], e)
            query = qp[p]
            sm[h, pl.ds(0, HALF), :] = (mix_of(h, 0, HALF, 0, ROWS) * nt(keys[:HALF], query)).astype(BF16)
            sm[h, pl.ds(HALF, HALF), pl.ds(HALF, HALF)] = (
                mix_of(h, HALF, HALF, HALF, HALF) * nt(keys[HALF:], query[HALF:])
            ).astype(BF16)
        return 0

    lax.fori_loop(0, PAIRS, scores_of, 0)

    def project_pair(n, slots, first, count, begin, end):
        cols = pl.ds(pl.multiple_of(n * 256, 256), 256)
        rows = pl.ds(first, count)
        total = None if begin else pacc[n, rows, :]
        for d in slots:
            if end:
                part = nn(gath[d, rows, :], w_turned[:, cols])
            else:
                part = nt(gath[d, rows, :], w4[d, cols, :])
            total = part if total is None else total + part
        if end:
            low = total.astype(BF16)
            dout[2 * n, rows, :] = low[:, :128]
            dout[2 * n + 1, rows, :] = low[:, 128:]
        else:
            pacc[n, rows, :] = total

    def project(*how):
        for n in range(PAIRS):
            project_pair(n, *how)

    def scaled_queries(p, e, first):
        rows = qT[p, e * 64:(e + 1) * 64, first:first + HALF].astype(F32)
        scaled = [
            (lam[LB + 1 + b, pl.ds(2 * p + e, 1), :][:, first:first + HALF] * rows).astype(BF16)
            for b in range(SEQ_BITS)
        ]
        return jnp.concatenate(scaled, axis=0)

    def level_first(p, _):
        for e in range(2):
            lgacc[p, e] = nn(scaled_queries(p, e, 0), dout[2 * p + e, 0:HALF, :])
        return 0

    def scale_rest(p, _):
        for e in range(2):
            rest[p, e] = scaled_queries(p, e, HALF)
        return 0

    def level_last(p):
        for e in range(2):
            grads = (lgacc[p, e] + nn(rest[p, e], dout[2 * p + e, HALF:ROWS, :])).astype(BF16)
            at = pl.ds(pl.multiple_of(p * 128 + e * 64, 64), 64)
            for b in range(SEQ_BITS):
                lg[b, at, :] = grads[b * 64:(b + 1) * 64, :]

    for load in loads[14:]:
        load.wait()
    project([y], 0, ROWS, True, False)
    arrive(s1[0])
    start(s1[1])
    turn(0)
    arrive(s1[1])
    start(s1[2])
    turn(1)
    project([left, right], 0, HALF, False, False)
    arrive(s1[2])
    start(s1[3])
    turn(2)

    turn(3)
    arrive(s1[3])
    parts = [zbuf[flipped(z, i, 3)].astype(F32) for i in range(8)]
    pair1 = parts[2] + parts[3]
    quad = (parts[4] + parts[5]) + (parts[6] + parts[7])
    xbuf[0] = ((parts[0] + parts[1]) + pair1 + quad).astype(BF16)
    s2 = start([remote(xbuf.at[0], xbuf.at[i], ss, sr, S2 + i - 1, x_peer(i)) for i in (1, 3)])
    state_low[1, mine, :] = parts[1].astype(BF16)
    state_low[2, mine, :] = pair1.astype(BF16)
    state_low[3, mine, :] = quad.astype(BF16)

    arrive(s2)
    s2 = start([remote(xbuf.at[1], xbuf.at[2], ss, sr, S2 + 1, x_peer(3))])
    project([left, right], HALF, HALF, False, False)
    lax.fori_loop(0, PAIRS, scale_rest, 0)
    for n in range(PAIRS):
        w_turned[:, n * 256:(n + 1) * 256] = w4[across, n * 256:(n + 1) * 256, :].T
    arrive(forwards[0])
    arrive(forwards[1])
    project([across], 0, HALF, False, True)
    lax.fori_loop(0, PAIRS, level_first, 0, unroll=True)

    arrive(forwards[2])
    project([across], HALF, CROWS, False, True)
    arrive(forwards[3])
    project([across], HALF + CROWS, CROWS, False, True)

    r0 = [[], []]

    def swap(i, levels):
        rows = pl.ds(pl.multiple_of((2 * (1 - c) + i) * 128, 128), 128)
        return start([
            remote(lg.at[1 + b, rows], rbh.at[b, pl.ds(i * 128, 128)], ss, sr, R0 + 5 * i + b, partner)
            for b in levels
        ])

    for i in range(2):
        level_last(2 * (1 - c) + i)
        r0[1] += swap(i, (4, 3))
    for i in range(2):
        r0[0] += swap(i, (0, 1, 2))
    for i in range(2):
        level_last(2 * c + i)

    def owned(at):
        return pl.ds(pl.multiple_of(at * SLICE, SLICE), SLICE)

    def chip_sum(first, count):
        levels = pl.ds(first, count)
        rsrc[levels] = (lg[pl.ds(1 + first, count), mine, :].astype(F32) + rbh[levels].astype(F32)).astype(BF16)

    def slice_of(i, level):
        return remote(rsrc.at[level, owned(flipped(z, i, 3))], rbuf.at[i, level], ss, sr, R1 + level, z_peer(i))

    def slices(count, level):
        some = rbuf.at[pl.ds(1, count), level]
        return remote(some, some, ss, sr, R1 + level, z_peer(1))

    set_bits = [(z // 2**b) % 2 for b in range(3)] + [x % 2, x // 2]

    def send_level(i, level):
        @pl.when(set_bits[level] == 1)
        def _():
            slice_of(i, level).start()

    for at, level in enumerate((4, 3)):
        arrive(r0[1][at::2])
        chip_sum(level, 1)
        for i in FAR_FIRST:
            send_level(i, level)
    arrive(r0[0])
    chip_sum(0, 3)
    for i in FAR_FIRST:
        for level in range(3):
            send_level(i, level)
    rbuf[0] = rsrc[:, owned(z), :]
    rb = start([remote(lg.at[0], rb0, ss, sr, R0 + 10, partner)])
    def attention(p, _):
        turned_k = kT[p]
        values = vp[p]
        query = qp[p]
        for e in range(2):
            h = 2 * p + e
            mine_q = masked(query, e)
            d = dout[h]
            mine_v = values[:, e * 128:(e + 1) * 128]
            low = (mix_of(h, 0, HALF, 0, ROWS) * nt(mine_v[:HALF], d)).astype(BF16)
            high = (mix_of(h, HALF, HALF, HALF, HALF) * nt(mine_v[HALF:], d[HALF:])).astype(BF16)
            key_low = nn(low, mine_q)
            key_high = nn(high, mine_q[HALF:])
            if e == 0:
                kacc[p, pl.ds(0, HALF), :] = key_low
                kacc[p, pl.ds(HALF, HALF), :] = key_high
            else:
                kacc[p, pl.ds(0, HALF), :] += key_low
                kacc[p, pl.ds(HALF, HALF), :] += key_high
            vacc[p, pl.ds(0, HALF), pl.ds(e * 128, 128)] = nn(sm[h, pl.ds(0, HALF), :], d)
            vacc[p, pl.ds(HALF, HALF), pl.ds(e * 128, 128)] = nn(
                sm[h, pl.ds(HALF, HALF), pl.ds(HALF, HALF)], d[HALF:]
            )
            own_k = turned_k[e * 64:(e + 1) * 64, :]
            line = nn(own_k[:, :HALF], low)
            line_high = nn(own_k[:, HALF:], high)
            qacc[p, pl.ds(e * 64, 64), :] = jnp.concatenate([line[:, :HALF], line[:, HALF:] + line_high], axis=1)
        return 0

    def read_states(p, _):
        lines = []
        for e in range(2):
            h = 2 * p + e
            at = pl.ds(pl.multiple_of(h * 64, 64), 64)
            read = nt(state_low[:, at, :].reshape(SEQ_BITS * 64, 128), dout[h])
            line = qacc[p, pl.ds(e * 64, 64), :]
            for b in range(SEQ_BITS):
                line = line + lam[LB + 1 + b, pl.ds(h, 1), :] * read[b * 64:(b + 1) * 64, :]
            lines.append(line)
        qo[p] = jnp.concatenate(lines, axis=0).T.astype(BF16)
        return 0

    lax.fori_loop(0, 2, attention, 0)
    for copy in sent:
        copy.wait_send()
    sent.clear()
    near = [remote(tsrc.at[0], tbuf.at[1, 0], ss, sr, R2, x_peer(1))]
    far = [remote(tsrc.at[1], tbuf.at[i, 1], ss, sr, R2 + i - 1, x_peer(i)) for i in (2, 3)]
    arrive(s2)
    for level, copies in ((4, far), (3, near)):
        @pl.when(set_bits[level] == 1)
        def _(level=level):
            slices(7, level).wait_recv()

        top = rbuf[0, level].astype(F32)
        for i in range(1, 8):
            top = top + rbuf[i, level].astype(F32)
        tsrc[level - 3] = top.astype(BF16)
        start_if(set_bits[level] == 1, copies)

    state_low[4, mine, :] = xbuf[1]
    state_low[5, mine, :] = (xbuf[2].astype(F32) + xbuf[3].astype(F32)).astype(BF16)
    s4 = start([
        remote(state_low.at[b, mine], state_low.at[b, mine], ss, sr, S4 + b - 1, partner) for b in range(1, SEQ_BITS)
    ])
    lax.fori_loop(2, 4, attention, 0)
    for level in range(3):
        @pl.when(set_bits[level] == 1)
        def _(level=level):
            slices(3, level).wait_recv()

        @pl.when(set_bits[level] == 0)
        def _(level=level):
            slices(4, level).wait_recv()
    arrive_if(x % 2 == 0, near)
    arrive_if(x // 2 == 0, far)
    outer = tbuf[1, 0].astype(F32) + tbuf[2, 1].astype(F32) + tbuf[3, 1].astype(F32)
    finals = pl.ds(pl.multiple_of(c * HALF + z * SLICE, SLICE), SLICE)
    for r in FAR_FIRST + (0,):
        total = outer
        for i in range(1, 8):
            total = total + rbuf[r ^ i, i.bit_length() - 1].astype(F32)
        rets[r] = total.astype(BF16)
        if r:
            remote(rets.at[r], rfin.at[finals], ss, sr, R3, z_peer(r)).start()
        remote(rets.at[r], rfin.at[finals], ss, sr, R3, z_other(r) if r else partner).start()
    rfin[finals, :] = rets[0]
    arrive(s4)
    lax.fori_loop(0, PAIRS, read_states, 0)
    for copy in sent:
        copy.wait_send()
    for level in range(5):
        @pl.when(set_bits[level] == 1)
        def _(level=level):
            slices(7, level).wait_send()
    for condition, copies in sent_if:
        @pl.when(condition)
        def _(copies=copies):
            for copy in copies:
                copy.wait_send()
    arrive(rb)
    every = rfin.at[pl.ds(0, 15 * SLICE)]
    last = remote(every, every, ss, sr, R3, partner)
    last.wait_recv()
    ret_ref[...] = (rfin[...].astype(F32) + rb0[...].astype(F32)).astype(BF16)
    last.wait_send()


def finish(back_ref, k_ref, v_ref, q_ref, kacc_ref, vacc_ref, qo_hbm, ko_hbm, vo_hbm, ko, vo, sem):
    copies = []

    def send(src, dst):
        copies.append(pltpu.make_async_copy(src, dst, sem.at[len(copies)]))
        copies[-1].start()

    for p in range(PAIRS):
        send(q_ref.at[p], qo_hbm.at[:, pl.ds(p * 128, 128)])
    zero = jnp.zeros((64, 128), BF16)
    for p in range(PAIRS):
        back = back_ref[pl.ds(p * 128, 128), :]
        spread = jnp.concatenate([
            jnp.concatenate([back[:64], zero], axis=1),
            jnp.concatenate([zero, back[64:]], axis=1),
        ], axis=0)
        vo[p] = (vacc_ref[p] + nn(k_ref[p], spread)).astype(BF16)
        send(vo.at[p], vo_hbm.at[:, pl.ds(p * 256, 256)])
        ko[p] = (kacc_ref[p] + nt(v_ref[p], spread)).astype(BF16)
        send(ko.at[p], ko_hbm.at[:, pl.ds(p * 128, 128)])
    for copy in copies:
        copy.wait()


def per_device(query_rows, key_rows, value_rows, out_grad, out_weight, level_codes, level_table):
    any_space = pl.BlockSpec(memory_space=pl.ANY)
    vmem = pl.BlockSpec(memory_space=pltpu.VMEM)
    scratch = [
        pltpu.VMEM((PAIRS, ROWS, 128), BF16),
        pltpu.VMEM((4, HEADS * DV, FEAT), BF16),
        pltpu.VMEM((4, ROWS, FEAT), BF16),
        pltpu.VMEM((HEADS, ROWS, DV), BF16),
        pltpu.VMEM((PAIRS, 128, ROWS), BF16),
        pltpu.VMEM((PAIRS, 128, ROWS), BF16),
        pltpu.VMEM((LB + 1 + SEQ_BITS, HEADS, ROWS), F32),
        pltpu.VMEM((ROWS // BLK, HEADS, ROWS), F32),
        pltpu.VMEM((HEADS, ROWS, ROWS), BF16),
        pltpu.VMEM((ROWS, 128), F32),
        pltpu.VMEM((ROWS, 128), F32),
        pltpu.VMEM((8, HALF, 128), BF16),
        pltpu.VMEM((4, HALF, 128), BF16),
        pltpu.VMEM((SEQ_BITS, ROWS, 128), BF16),
        pltpu.VMEM((SEQ_BITS, ROWS, 128), BF16),
        pltpu.VMEM((ROWS, 128), BF16),
        pltpu.VMEM((5, HALF, 128), BF16),
        pltpu.VMEM((5, HALF, 128), BF16),
        pltpu.VMEM((8, 5, SLICE, 128), BF16),
        pltpu.VMEM((2, SLICE, 128), BF16),
        pltpu.VMEM((4, 2, SLICE, 128), BF16),
        pltpu.VMEM((8, SLICE, 128), BF16),
        pltpu.VMEM((ROWS, 128), BF16),
        pltpu.VMEM((4, ROWS, 256), F32),
        pltpu.VMEM((PAIRS, 2, SEQ_BITS * 64, 128), F32),
        pltpu.VMEM((PAIRS, 2, SEQ_BITS * 64, HALF), BF16),
        pltpu.VMEM((PAIRS, 128, ROWS), F32),
        pltpu.VMEM((FEAT, HEADS * DV), BF16),
        pltpu.VMEM((12, HEADS, ROWS), jnp.int32),
        pltpu.VMEM((HEADS, 16), F32),
        pltpu.SemaphoreType.DMA((19,)),
        pltpu.SemaphoreType.DMA((16,)),
        pltpu.SemaphoreType.DMA((16,)),
        pltpu.SemaphoreType.DMA((N_SEM,)),
        pltpu.SemaphoreType.DMA((N_SEM,)),
    ]
    inputs = [
        pltpu.with_memory_space_constraint(array, pltpu.HBM)
        for array in (query_rows, key_rows, value_rows, out_grad, out_weight, level_codes, level_table)
    ]
    queries, keys, values, returned, key_pairs, value_pairs = pl.pallas_call(
        kernel,
        out_shape=(
            pltpu.VMEM((PAIRS, ROWS, 128), BF16),
            pltpu.VMEM((PAIRS, ROWS, 128), F32),
            pltpu.VMEM((PAIRS, ROWS, 256), F32),
            pltpu.VMEM((ROWS, 128), BF16),
            pltpu.VMEM((PAIRS, ROWS, 128), BF16),
            pltpu.VMEM((PAIRS, ROWS, 256), BF16),
        ),
        in_specs=[any_space] * 7,
        out_specs=(vmem,) * 6,
        scratch_shapes=scratch,
        compiler_params=pltpu.CompilerParams(
            collective_id=0, has_side_effects=True, vmem_limit_bytes=40 * 1024 * 1024
        ),
        cost_estimate=pl.CostEstimate(flops=8_000_000_000, bytes_accessed=12_000_000, transcendentals=0),
    )(*inputs)
    return pl.pallas_call(
        finish,
        out_shape=(
            jax.ShapeDtypeStruct((ROWS, HEADS * DK), BF16),
            jax.ShapeDtypeStruct((ROWS, HEADS * DK), BF16),
            jax.ShapeDtypeStruct((ROWS, HEADS * DV), BF16),
        ),
        in_specs=[vmem] * 6,
        out_specs=(any_space,) * 3,
        scratch_shapes=[
            pltpu.VMEM((PAIRS, ROWS, 128), BF16),
            pltpu.VMEM((PAIRS, ROWS, 256), BF16),
            pltpu.SemaphoreType.DMA((3 * PAIRS,)),
        ],
        compiler_params=pltpu.CompilerParams(vmem_limit_bytes=16 * 1024 * 1024),
        cost_estimate=pl.CostEstimate(flops=500_000_000, bytes_accessed=8_000_000, transcendentals=0),
    )(returned, key_pairs, value_pairs, queries, keys, values)


def solution(mesh):
    return jax.shard_map(
        per_device,
        mesh=mesh,
        in_specs=(
            P("seq", "head"),
            P("seq", "head"),
            P("seq", "head"),
            P("seq", "head"),
            P("head", None),
            P(None, "head", "seq"),
            P("head", None),
        ),
        out_specs=(P("seq", "head"), P("seq", "head"), P("seq", "head")),
        check_vma=False,
    )
```
